32 devices in a mesh: dp: 8 (over z, x), tensor: 4 (over y, core).
Axes of the slice: x: 2, y: 2, z: 4, core: 2. Of those that a mesh axis runs over, the one named last changes fastest.
Arguments:
- tokens: bfloat16 [8192, 768], P(('dp', 'tensor')), may hold values from -6 to 6
- final_output_gradient: bfloat16 [8192, 768], P(('dp', 'tensor')), may hold values from -6 to 6
- lengths: int32 [8, 32], P('dp'), may hold values from 0 to 512, as said below
- query_key_value_weight: bfloat16 [2, 3, 768, 768], P(None, None, 'dp', 'tensor'), may hold values from -0.21875 to 0.21875
- output_projection_weight: bfloat16 [2, 768, 768], P(None, 'dp', 'tensor'), may hold values from -0.625 to 0.625
- biases: float32 [2, 6, 768], replicated, may hold values from -2.5 to 2.5
- frozen_norm_gains: float32 [2, 2, 768], replicated, may hold values from 0.5 to 1.5
- feedforward_in_weight: bfloat16 [2, 768, 3072], P(None, None, 'tensor'), may hold values from -0.21875 to 0.21875
- feedforward_bias: bfloat16 [2, 3072], P(None, 'tensor'), may hold values from -2.5 to 2.5
- feedforward_out_weight: bfloat16 [2, 3072, 768], P(None, 'tensor'), may hold values from -0.109375 to 0.109375
- adapter_down_weights: bfloat16 [2, 2, 768, 8], replicated, may hold values from -0.21875 to 0.21875
- adapter_up_weights: bfloat16 [2, 2, 8, 768], replicated, may hold values from -2 to 2
Outputs:
- activations: bfloat16 [8192, 768], P(('dp', 'tensor'))
- input_grad: bfloat16 [8192, 768], P(('dp', 'tensor'))
- lora_a_grad: float32 [2, 2, 768, 8], replicated
- lora_b_grad: float32 [2, 2, 8, 768], replicated
The draws below stay inside these ranges and needn't reach their ends.
Inputs may be any that keep to these rules, and one draw needn't show every extreme that they name: Row g lists the lengths of the sequences packed in order into the 1024 rows of group g; the nonzero entries form a prefix whose sum is at most 1024, the rows past it being padding; a length of 512 occurs in every draw.
All inputs are finite; a program needn't handle non-finite values.
Results may differ from the reference program's by a relative error of at most 0.035.
Values may be sent and summed in bfloat16 or wider, within the bound.
No kernel may reach another device: no remote copies, remote signals or barrier semaphores. Data moves between devices by JAX's collectives and lax.ppermute only.
A program may use at most 128 MiB of HBM per device.

```python
import jax
import jax.numpy as jnp
from jax import lax

MODEL_WIDTH = 768
HEADS = 12
HEAD_DIM = 64
FF = 3072
ADAPTER_RANK = 8
ENCODER_LAYERS = 2
MAXLEN = 512
GROUP = 1024
GROUPS = 8
SLOTS = 32
TOKENS = 8192


def draw_lengths(key, part):
    key = jax.random.fold_in(key, 17)
    short_key, flag_key, pick_key = jax.random.split(key, 3)
    least_len = max(MAXLEN // 32, 1)
    short_len = jax.random.randint(short_key, (GROUPS, SLOTS), least_len, MAXLEN // 4 + 1, dtype=jnp.int32)
    flagged = jax.random.randint(flag_key, (GROUPS,), 0, 8, dtype=jnp.int32) == 0
    chosen = jax.random.randint(pick_key, (), 0, GROUPS, dtype=jnp.int32)
    flagged = flagged | (jnp.arange(GROUPS, dtype=jnp.int32) == chosen)
    long_count = max(GROUP // MAXLEN - 1, 1)
    slot_index = jnp.arange(SLOTS, dtype=jnp.int32)
    raw_len = jnp.where(flagged[:, None] & (slot_index[None, :] < long_count), MAXLEN, short_len)
    slot_ends = jnp.cumsum(raw_len, axis=1)
    return jnp.where(slot_ends <= GROUP, raw_len, 0).astype(jnp.int32)


def steps_of(rng, dims, pieces, smallest, high):
    def one(axis_at, parts):
        draws = jax.random.uniform(jax.random.fold_in(jax.random.fold_in(rng, 6), axis_at), (parts,), jnp.float32, smallest / len(pieces), high / len(pieces))
        return jnp.repeat(jnp.exp(draws), dims[axis_at] // parts).reshape((-1,) + (1,) * (len(dims) - axis_at - 1))

    level = one(*pieces[0])
    for cut in pieces[1:]:
        level = level * one(*cut)
    return level


def scatter_about(key, shape, deviation, bound, cuts=(), held_as=jnp.bfloat16):
    entries = jax.random.normal(key, shape, jnp.float32) * deviation
    if len(cuts) > 0:
        entries = steps_of(key, shape, cuts, -0.22, 0.18) * entries
    return jnp.clip(entries, min=-bound, max=bound).astype(held_as)


def setup_inputs(seed: int = 0) -> dict:
    key_of = jax.random.split(jax.random.key(seed), 13)
    tokens = scatter_about(key_of[0], (TOKENS, MODEL_WIDTH), 1.0, 6.0, ((0, 32),))
    final_output_gradient = scatter_about(key_of[1], (TOKENS, MODEL_WIDTH), 1.0, 6.0, ((0, 32),))
    lengths = draw_lengths(jax.random.fold_in(key_of[12], 71), 0)
    query_key_value_weight = scatter_about(key_of[3], (ENCODER_LAYERS, 3, MODEL_WIDTH, MODEL_WIDTH), MODEL_WIDTH ** -0.5, 0.21875, ((2, 8), (3, 4)))
    output_projection_weight = scatter_about(key_of[4], (ENCODER_LAYERS, MODEL_WIDTH, MODEL_WIDTH), (MODEL_WIDTH // 8) ** -0.5, 0.625, ((1, 8), (2, 4)))
    biases = scatter_about(key_of[5], (ENCODER_LAYERS, 6, MODEL_WIDTH), 0.5, 2.5, (), jnp.float32)
    frozen_norm_gains = jnp.clip(1.0 + 0.1 * jax.random.normal(key_of[6], (ENCODER_LAYERS, 2, MODEL_WIDTH), jnp.float32), 0.5, 1.5)
    feedforward_in_weight = scatter_about(key_of[7], (ENCODER_LAYERS, MODEL_WIDTH, FF), MODEL_WIDTH ** -0.5, 0.21875, ((2, 4),))
    feedforward_bias = scatter_about(key_of[8], (ENCODER_LAYERS, FF), 0.5, 2.5, ((1, 4),))
    feedforward_out_weight = scatter_about(key_of[9], (ENCODER_LAYERS, FF, MODEL_WIDTH), FF ** -0.5, 0.109375, ((1, 4),))
    adapter_down_weights = scatter_about(key_of[10], (ENCODER_LAYERS, 2, MODEL_WIDTH, ADAPTER_RANK), MODEL_WIDTH ** -0.5, 0.21875)
    adapter_up_weights = scatter_about(key_of[11], (ENCODER_LAYERS, 2, ADAPTER_RANK, MODEL_WIDTH), ADAPTER_RANK ** -0.5, 2.0)
    return {"tokens": tokens, "final_output_gradient": final_output_gradient, "lengths": lengths, "query_key_value_weight": query_key_value_weight, "output_projection_weight": output_projection_weight, "biases": biases, "frozen_norm_gains": frozen_norm_gains, "feedforward_in_weight": feedforward_in_weight, "feedforward_bias": feedforward_bias, "feedforward_out_weight": feedforward_out_weight, "adapter_down_weights": adapter_down_weights, "adapter_up_weights": adapter_up_weights}


@jax.custom_vjp
def low_rank_state(v):
    return lax.optimization_barrier(v.astype(jnp.bfloat16)).astype(jnp.float32)

@jax.custom_vjp
def low_rank_gradient(v):
    return v

def low_keep(v):
    return (low_rank_state(v), None)

def low_pass(kept, grad):
    return (grad,)

def back_keep(v):
    return (v, None)

def back_low(kept, grad):
    return (low_rank_state(grad),)
low_rank_state.defvjp(low_keep, low_pass)
low_rank_gradient.defvjp(back_keep, back_low)
epsilon = 1e-05
adapter_scale = 2.0
masked_score = -1000000000.0
exact_prec = lax.Precision.HIGHEST

def normalize(row_data, gain_row, shift_row):
    row_mean = lax.optimization_barrier(jnp.mean(row_data, axis=-1, keepdims=True))
    centered = row_data - row_mean
    variance = lax.optimization_barrier(jnp.mean(centered * centered, axis=-1, keepdims=True))
    return centered * lax.rsqrt(variance + epsilon) * gain_row + shift_row

def segment_of(lengths_row, group_len):
    seg_ends = jnp.cumsum(lengths_row)
    position = jnp.arange(group_len, dtype=jnp.int32)
    return lax.optimization_barrier(jnp.sum((seg_ends[None, :] <= position[:, None]).astype(jnp.int32), axis=1))

def matrix_product(left_op, right_op):
    return jnp.dot(left_op, right_op, precision=exact_prec)

def attention_group(rows_of_queries, key_rows, rows_of_values, segment):
    group_len = rows_of_queries.shape[0]
    block_len = min(512, group_len)
    scale = HEAD_DIM ** (-0.5)

    def one_block(block_index):
        row_start = block_index * block_len
        query_block = lax.dynamic_slice_in_dim(rows_of_queries, row_start, block_len, 0)
        segment_block = lax.dynamic_slice_in_dim(segment, row_start, block_len, 0)
        scores = jnp.einsum('qhd,khd->hqk', query_block, key_rows, precision=exact_prec) * scale
        scores = jnp.where((segment_block[:, None] == segment[None, :])[None], scores, masked_score)
        scores = low_rank_gradient(scores)
        top_score = lax.optimization_barrier(jnp.max(scores, axis=-1, keepdims=True))
        weights = jnp.exp(scores - top_score)
        prob_low = low_rank_state(weights / lax.optimization_barrier(jnp.sum(weights, axis=-1, keepdims=True)))
        return jnp.einsum('hqk,khd->qhd', prob_low, rows_of_values, precision=exact_prec)
    context = lax.map(jax.checkpoint(one_block), jnp.arange(group_len // block_len, dtype=jnp.int32))
    return context.reshape(group_len, -1)

def encoder_layer(layer_in, current_layer_index, frozen, adapter_a, adapter_up_matrix):
    query_key_value_weight, output_projection_weight, biases, frozen_norm_gains, feedforward_in_weight, feedforward_bias, feedforward_out_weight, segments = frozen
    head_projections = query_key_value_weight[current_layer_index]

    def split_heads(block_data):
        return block_data.reshape(GROUP, HEADS, HEAD_DIM)

    def group_step(group_args):
        segment_group_rows, segment = group_args
        query_down_weight = low_rank_state(matrix_product(segment_group_rows, adapter_a[current_layer_index, 0]))
        value_down_weight = low_rank_state(matrix_product(segment_group_rows, adapter_a[current_layer_index, 1]))
        rows_of_queries = low_rank_gradient(low_rank_state(matrix_product(segment_group_rows, head_projections[0]) + biases[current_layer_index, 0] + adapter_scale * matrix_product(query_down_weight, adapter_up_matrix[current_layer_index, 0])))
        key_rows = low_rank_gradient(low_rank_state(matrix_product(segment_group_rows, head_projections[1])))
        rows_of_values = low_rank_gradient(low_rank_state(matrix_product(segment_group_rows, head_projections[2]) + biases[current_layer_index, 1] + adapter_scale * matrix_product(value_down_weight, adapter_up_matrix[current_layer_index, 1])))
        context = low_rank_gradient(low_rank_state(attention_group(split_heads(rows_of_queries), split_heads(key_rows), split_heads(rows_of_values), segment)))
        attn_out = low_rank_gradient(matrix_product(context, output_projection_weight[current_layer_index].T))
        first_sum = segment_group_rows + attn_out + biases[current_layer_index, 2]
        normed = normalize(first_sum, frozen_norm_gains[current_layer_index, 0], biases[current_layer_index, 3])
        pre_act = low_rank_gradient(matrix_product(low_rank_state(normed), feedforward_in_weight[current_layer_index]) + feedforward_bias[current_layer_index])
        hidden = low_rank_state(jax.nn.gelu(pre_act, approximate=False))
        ffn_rows = low_rank_gradient(matrix_product(hidden, feedforward_out_weight[current_layer_index]))
        second_sum = normed + ffn_rows + biases[current_layer_index, 4]
        return normalize(second_sum, frozen_norm_gains[current_layer_index, 1], biases[current_layer_index, 5])
    grouped = layer_in.reshape(GROUPS, GROUP, MODEL_WIDTH)
    final_result = lax.map(jax.checkpoint(group_step), (grouped, segments))
    return final_result.reshape(-1, MODEL_WIDTH)

def reference(tokens, final_output_gradient, lengths, query_key_value_weight, output_projection_weight, biases, frozen_norm_gains, feedforward_in_weight, feedforward_bias, feedforward_out_weight, adapter_down_weights, adapter_up_weights):

    def group_segment(lengths_row):
        return segment_of(lengths_row, GROUP)
    segments = jax.vmap(group_segment)(lengths)
    frozen = (query_key_value_weight.astype(jnp.float32), output_projection_weight.astype(jnp.float32), biases.astype(jnp.float32), frozen_norm_gains.astype(jnp.float32), feedforward_in_weight.astype(jnp.float32), feedforward_bias.astype(jnp.float32), feedforward_out_weight.astype(jnp.float32), segments)

    def forward_pass(layer_in, adapter_a, adapter_up_matrix):
        hidden_state = layer_in
        for current_layer_index in range(ENCODER_LAYERS):
            hidden_state = encoder_layer(hidden_state, current_layer_index, frozen, adapter_a, adapter_up_matrix)
            if current_layer_index + 1 < ENCODER_LAYERS:
                hidden_state = low_rank_state(hidden_state)
        return hidden_state
    final_result, reverse_mapping = jax.vjp(forward_pass, tokens.astype(jnp.float32), adapter_down_weights.astype(jnp.float32), adapter_up_weights.astype(jnp.float32))
    grad_in, grad_a, grad_b = reverse_mapping(final_output_gradient.astype(jnp.float32))
    return (final_result.astype(jnp.bfloat16), grad_in.astype(jnp.bfloat16), grad_a, grad_b)
```

```python
import functools

import jax
import jax.numpy as jnp
from jax import lax
from jax.experimental import pallas as pl
from jax.experimental.pallas import tpu as pltpu
from jax.sharding import PartitionSpec as P

MODEL_WIDTH = 768
HEAD_DIM = 64
ADAPTER_RANK = 8
ENCODER_LAYERS = 2
SET_HEADS = 6
SET_COLS = SET_HEADS * HEAD_DIM
KEY_BLOCK = 128
EPSILON = 1e-05
MASKED = -1000000000.0
VMEM_LIMIT = 56 * 1024 * 1024

F32 = jnp.float32
BF16 = jnp.bfloat16


def dot_nn(a, b):
    return lax.dot_general(a, b, (((1,), (0,)), ((), ())), preferred_element_type=F32)


def dot_nt(a, b):
    return lax.dot_general(a, b, (((1,), (1,)), ((), ())), preferred_element_type=F32)


def dot_tn(a, b):
    return lax.dot_general(a, b, (((0,), (0,)), ((), ())), preferred_element_type=F32)


def aligned(start, size):
    return pl.ds(pl.multiple_of(start, size), size)


def range_of_rows(meta_ref, slots, first_row, rows, group_len):
    row = first_row + lax.broadcasted_iota(jnp.int32, (1, rows), 1)
    start = jnp.zeros((1, rows), jnp.int32)
    end = jnp.full((1, rows), group_len, jnp.int32)
    for s in range(slots):
        e = meta_ref[s]
        start = jnp.where(e <= row, jnp.maximum(start, e), start)
        end = jnp.where(e > row, jnp.minimum(end, e), end)
    return start, end


def scalar_range(meta_ref, slots, first_row, last_row, group_len):
    low = jnp.int32(0)
    high = jnp.int32(group_len)
    for s in range(slots):
        e = meta_ref[s]
        low = jnp.where(e <= first_row, jnp.maximum(low, e), low)
        high = jnp.where(e > last_row, jnp.minimum(high, e), high)
    return low, high


def piece_copies(pieces, source_of, target_of, sem, shard):
    out = []
    rows = MODEL_WIDTH // len(pieces)
    for k, piece in enumerate(pieces):
        if len(pieces) == 1:
            target = target_of(pl.ds(0, rows))
        else:
            target = target_of(aligned(jnp.bitwise_xor(shard, k) * rows, rows))
        out.append(pltpu.make_async_copy(source_of(piece), target, sem))
    return out


def attention_forward_kernel(n_pieces, slots, group_len, meta, *refs):
    x_refs = refs[:4]
    pieces = refs[4 : 4 + n_pieces]
    adapter, up, bias = refs[4 + n_pieces : 7 + n_pieces]
    q_out, k_out, v_out, lse_out, c_out, own_out, sib_out = refs[7 + n_pieces : 14 + n_pieces]
    xs, w, qm, down, vt, acc, x_sem, w_sem = refs[14 + n_pieces :]
    rows_dev = x_refs[0].shape[0]
    chip_rows = 2 * rows_dev
    t = meta[slots]
    shard = meta[slots + 1]
    core = jnp.bitwise_and(t, 1)
    chip0 = (t - core) * rows_dev

    x_copies = [
        pltpu.make_async_copy(
            x_refs[j], xs.at[aligned(jnp.bitwise_xor(t, j) * rows_dev, rows_dev)], x_sem.at[j]
        )
        for j in range(4)
    ]
    for c in x_copies:
        c.start()
    w_copies = [
        piece_copies(pieces, lambda p, m=m: p.at[m], lambda r, m=m: w.at[m, r], w_sem.at[m], shard)
        for m in range(4)
    ]
    for group in w_copies:
        for c in group:
            c.start()
    low, high = scalar_range(meta, slots, chip0, chip0 + chip_rows - 1, group_len)
    for c in x_copies:
        c.wait()
    for m in (1, 2):
        for c in w_copies[m]:
            c.wait()

    def project_block(b, _):
        rows = aligned(b * rows_dev, rows_dev)
        xb = xs[rows]
        db = dot_nn(xb, adapter[...]).astype(BF16)
        down[rows] = db
        k_out[rows] = dot_nn(xb, w[1]).astype(BF16)
        vb = (dot_nn(xb, w[2]) + dot_nn(db, up[1]) + bias[1:2]).astype(BF16)
        v_out[rows] = vb
        vb_t = vb.T
        for half in range(rows_dev // KEY_BLOCK):
            vt[b * (rows_dev // KEY_BLOCK) + half] = vb_t[:, half * KEY_BLOCK : (half + 1) * KEY_BLOCK]
        return 0

    lax.fori_loop(low // rows_dev, (high + rows_dev - 1) // rows_dev, project_block, 0)

    for c in w_copies[0]:
        c.wait()
    lane = lax.broadcasted_iota(jnp.int32, (rows_dev, 128), 1)
    for qb in range(2):
        rows = aligned(chip0 + qb * rows_dev, rows_dev)
        here = pl.ds(qb * rows_dev, rows_dev)
        qv = (dot_nn(xs[rows], w[0]) + dot_nn(down[rows], up[0]) + bias[0:1]) * HEAD_DIM**-0.5
        qv = qv.astype(BF16)
        q_out[here] = qv
        for h in range(SET_HEADS):
            pair = qv[:, (h // 2) * 128 : (h // 2 + 1) * 128]
            keep = (lane < HEAD_DIM) if h % 2 == 0 else (lane >= HEAD_DIM)
            qm[h] = jnp.where(keep, pair, jnp.zeros_like(pair))

        first = chip0 + qb * rows_dev
        klow, khigh = scalar_range(meta, slots, first, first + rows_dev - 1, group_len)
        q_start, q_end = range_of_rows(meta, slots, first, rows_dev, group_len)
        acc[...] = jnp.zeros_like(acc)

        def key_step(kb, carry, q_start=q_start, q_end=q_end):
            tops, sums = carry
            keys = aligned(kb * KEY_BLOCK, KEY_BLOCK)
            kpos = kb * KEY_BLOCK + lax.broadcasted_iota(jnp.int32, (KEY_BLOCK, rows_dev), 0)
            mask = jnp.where((kpos >= q_start) & (kpos < q_end), 0.0, MASKED)
            new_tops, new_sums = [], []
            for h in range(SET_HEADS):
                s = dot_nt(k_out[keys, (h // 2) * 128 : (h // 2 + 1) * 128], qm[h]) + mask
                top = jnp.maximum(tops[h], jnp.max(s, axis=0, keepdims=True))
                p = jnp.exp(s - top)
                fade = jnp.exp(tops[h] - top)
                new_tops.append(top)
                new_sums.append(sums[h] * fade + jnp.sum(p, axis=0, keepdims=True))
                cols = pl.ds(h * HEAD_DIM, HEAD_DIM)
                acc[cols] = acc[cols] * fade + dot_nn(
                    vt[kb, h * HEAD_DIM : (h + 1) * HEAD_DIM, :], p.astype(BF16)
                )
            return tuple(new_tops), tuple(new_sums)

        init = (
            tuple(jnp.full((1, rows_dev), -3e38, F32) for _ in range(SET_HEADS)),
            tuple(jnp.zeros((1, rows_dev), F32) for _ in range(SET_HEADS)),
        )
        tops, sums = lax.fori_loop(
            klow // KEY_BLOCK, (khigh + KEY_BLOCK - 1) // KEY_BLOCK, key_step, init
        )
        for h in range(SET_HEADS):
            cols = pl.ds(h * HEAD_DIM, HEAD_DIM)
            acc[cols] = acc[cols] / sums[h]
            lse_out[h : h + 1, qb * rows_dev : (qb + 1) * rows_dev] = tops[h] + jnp.log(sums[h])
        c_out[here] = acc[...].T.astype(BF16)

    for c in w_copies[3]:
        c.wait()
    own_out[...] = dot_nt(c_out[aligned(core * rows_dev, rows_dev)], w[3])
    sib_out[...] = dot_nt(c_out[aligned((1 - core) * rows_dev, rows_dev)], w[3]).astype(BF16)


ANY = pl.BlockSpec(memory_space=pl.ANY)
SMEM = pl.BlockSpec(memory_space=pltpu.SMEM)
VMEM = pl.BlockSpec(memory_space=pltpu.VMEM)


def estimate(flops, nbytes):
    return pl.CostEstimate(flops=flops, bytes_accessed=nbytes, transcendentals=0)


def attention_forward(meta, xs, pieces, adapter, up, bias):
    rows = xs[0].shape[0]
    group = 4 * rows
    slots = meta.shape[0] - 2
    n = len(pieces)
    return pl.pallas_call(
        functools.partial(attention_forward_kernel, n, slots, group),
        out_shape=(
            jax.ShapeDtypeStruct((2 * rows, SET_COLS), BF16),
            jax.ShapeDtypeStruct((group, SET_COLS), BF16),
            jax.ShapeDtypeStruct((group, SET_COLS), BF16),
            jax.ShapeDtypeStruct((8, 2 * rows), F32),
            jax.ShapeDtypeStruct((2 * rows, SET_COLS), BF16),
            jax.ShapeDtypeStruct((rows, MODEL_WIDTH), F32),
            jax.ShapeDtypeStruct((rows, MODEL_WIDTH), BF16),
        ),
        in_specs=[SMEM] + [ANY] * (4 + n) + [VMEM] * 3,
        out_specs=[VMEM] * 7,
        scratch_shapes=[
            pltpu.VMEM((group, MODEL_WIDTH), BF16),
            pltpu.VMEM((4, MODEL_WIDTH, SET_COLS), BF16),
            pltpu.VMEM((SET_HEADS, rows, 128), BF16),
            pltpu.VMEM((group, 128), BF16),
            pltpu.VMEM((group // KEY_BLOCK, SET_COLS, KEY_BLOCK), BF16),
            pltpu.VMEM((SET_COLS, rows), F32),
            pltpu.SemaphoreType.DMA((4,)),
            pltpu.SemaphoreType.DMA((4,)),
        ],
        compiler_params=pltpu.CompilerParams(vmem_limit_bytes=VMEM_LIMIT),
        cost_estimate=estimate(6_000_000_000, 8_000_000),
        name="attention_forward",
    )(meta, *xs, *pieces, adapter, up, bias)


def attention_backward_kernel(n_pieces, slots, group_len, meta, *refs):
    x_refs = refs[:4]
    pieces = refs[4 : 4 + n_pieces]
    g_low, g_sib, g_own, q_in, k_in, v_in, lse, c_in, adapter, up = refs[4 + n_pieces : 14 + n_pieces]
    out0, out1, out2, out3, grads = refs[14 + n_pieces : 19 + n_pieces]
    xs, w, gl, gc, gcm, qm, kt, gk, gv, gqt, down, ga, gb, x_sem, w_sem = refs[19 + n_pieces :]
    rows_dev = x_refs[0].shape[0]
    chip_rows = 2 * rows_dev
    t = meta[slots]
    shard = meta[slots + 1]
    core = jnp.bitwise_and(t, 1)
    chip0 = (t - core) * rows_dev
    w_copies = [
        piece_copies(pieces, lambda p, m=m: p.at[m], lambda r, m=m: w.at[m, r], w_sem.at[m], shard)
        for m in range(4)
    ]
    for m in (3, 0, 1, 2):
        for c in w_copies[m]:
            c.start()
    x_copies = [
        pltpu.make_async_copy(
            x_refs[j], xs.at[aligned(jnp.bitwise_xor(t, j) * rows_dev, rows_dev)], x_sem.at[j]
        )
        for j in range(4)
    ]
    for c in x_copies:
        c.start()
    low, high = scalar_range(meta, slots, chip0, chip0 + chip_rows - 1, group_len)
    block_low = low // rows_dev
    block_high = (high + rows_dev - 1) // rows_dev

    gl[aligned(core * rows_dev, rows_dev)] = g_low[...]
    gl[aligned((1 - core) * rows_dev, rows_dev)] = g_sib[...]
    for c in w_copies[3]:
        c.wait()
    gc[...] = dot_nn(gl[...], w[3]).astype(BF16)
    for c in x_copies:
        c.wait()

    def prepare_block(b, _):
        rows = aligned(b * rows_dev, rows_dev)
        down[rows] = dot_nn(xs[rows], adapter[...]).astype(BF16)
        kb_t = k_in[rows].T
        for half in range(rows_dev // KEY_BLOCK):
            kt[b * (rows_dev // KEY_BLOCK) + half] = kb_t[:, half * KEY_BLOCK : (half + 1) * KEY_BLOCK]
        gk[rows] = jnp.zeros((rows_dev, SET_COLS), F32)
        gv[rows] = jnp.zeros((rows_dev, SET_COLS), F32)
        return 0

    lax.fori_loop(block_low, block_high, prepare_block, 0)

    pick = (
        lax.broadcasted_iota(jnp.int32, (8, SET_COLS), 1) // HEAD_DIM
        == lax.broadcasted_iota(jnp.int32, (8, SET_COLS), 0)
    ).astype(BF16)
    lane = lax.broadcasted_iota(jnp.int32, (rows_dev, 128), 1)
    for qb in range(2):
        here = pl.ds(qb * rows_dev, rows_dev)
        cols_here = slice(qb * rows_dev, (qb + 1) * rows_dev)
        product = gc[here].astype(F32) * c_in[here].astype(F32)
        product_high = product.astype(BF16)
        product_low = (product - product_high.astype(F32)).astype(BF16)
        delta = dot_nt(pick, product_high) + dot_nt(pick, product_low)
        for h in range(SET_HEADS):
            cols = slice((h // 2) * 128, (h // 2 + 1) * 128)
            keep = (lane < HEAD_DIM) if h % 2 == 0 else (lane >= HEAD_DIM)
            pair = q_in[here, cols]
            qm[h] = jnp.where(keep, pair, jnp.zeros_like(pair))
            pair = gc[here, cols]
            gcm[h] = jnp.where(keep, pair, jnp.zeros_like(pair))
        first = chip0 + qb * rows_dev
        klow, khigh = scalar_range(meta, slots, first, first + rows_dev - 1, group_len)
        q_start, q_end = range_of_rows(meta, slots, first, rows_dev, group_len)
        gqt[...] = jnp.zeros_like(gqt)

        def key_step(kb, _, q_start=q_start, q_end=q_end, delta=delta, cols_here=cols_here):
            keys = aligned(kb * KEY_BLOCK, KEY_BLOCK)
            kpos = kb * KEY_BLOCK + lax.broadcasted_iota(jnp.int32, (KEY_BLOCK, rows_dev), 0)
            mask = jnp.where((kpos >= q_start) & (kpos < q_end), 0.0, MASKED)
            for pair in range(SET_HEADS // 2):
                cols = slice(pair * 128, (pair + 1) * 128)
                kp = k_in[keys, cols]
                vp = v_in[keys, cols]
                gk_sum = gk[keys, cols]
                gv_sum = gv[keys, cols]
                for h in (2 * pair, 2 * pair + 1):
                    s = dot_nt(kp, qm[h]) + mask
                    p = jnp.exp(s - lse[h : h + 1, cols_here])
                    gp = dot_nt(vp, gcm[h])
                    gs = (p * (gp - delta[h : h + 1])).astype(BF16)
                    head = slice(h * HEAD_DIM, (h + 1) * HEAD_DIM)
                    gqt[head] += dot_nn(kt[kb, head, :], gs)
                    gk_sum = gk_sum + dot_nn(gs, qm[h])
                    gv_sum = gv_sum + dot_nn(p.astype(BF16), gcm[h])
                gk[keys, cols] = gk_sum
                gv[keys, cols] = gv_sum
            return 0

        lax.fori_loop(klow // KEY_BLOCK, (khigh + KEY_BLOCK - 1) // KEY_BLOCK, key_step, 0)
        gc[here] = (gqt[...].T * HEAD_DIM**-0.5).astype(BF16)

    for m in (0, 1, 2):
        for c in w_copies[m]:
            c.wait()
    ga[...] = jnp.zeros_like(ga)
    gb[...] = jnp.zeros_like(gb)

    def input_gradient(b):
        rows = aligned(b * rows_dev, rows_dev)
        gvb = gv[rows].astype(BF16)
        gd = dot_nt(gvb, up[1])
        g = dot_nt(gk[rows].astype(BF16), w[1]) + dot_nt(gvb, w[2])
        gb[1] += dot_tn(down[rows], gvb)
        return g, gd

    def query_gradient(b):
        gq = gc[aligned(b * rows_dev - chip0, rows_dev)]
        gd = dot_nt(gq, up[0])
        g = dot_nt(gq, w[0])
        gb[0] += dot_tn(down[aligned(b * rows_dev, rows_dev)], gq)
        return g, gd

    def add_adapter(b, g, gd):
        gd = gd.astype(BF16)
        ga[...] += dot_tn(gd, xs[aligned(b * rows_dev, rows_dev)])
        return g + dot_nt(gd, adapter[...])

    for j, out in ((2, out2), (3, out3)):
        b = jnp.bitwise_xor(t, j)
        used = (b >= block_low) & (b < block_high)

        @pl.when(used)
        def _(b=b, out=out):
            g, gd = input_gradient(b)
            out[...] = add_adapter(b, g, gd).astype(BF16)

        @pl.when(jnp.logical_not(used))
        def _(out=out):
            out[...] = jnp.zeros_like(out)

    for j, out in ((1, out1), (0, out0)):
        b = jnp.bitwise_xor(t, j)
        g, gd = input_gradient(b)
        gq, gdq = query_gradient(b)
        g = add_adapter(b, g + gq, gd + gdq)
        out[...] = (g + g_own[...] if j == 0 else g).astype(out.dtype)

    grads[0:16] = ga[0:16]
    for c in range(2):
        cols = slice(c * SET_COLS, (c + 1) * SET_COLS)
        mine = jnp.where(core == c, 2.0, 0.0)
        grads[16:24, cols] = gb[0, 0:8] * mine
        grads[24:32, cols] = gb[1, 8:16] * mine


def attention_backward(meta, xs, pieces, g_low, g_sib, g_own, saved, adapter, up):
    rows = xs[0].shape[0]
    group = 4 * rows
    slots = meta.shape[0] - 2
    n = len(pieces)
    block = jax.ShapeDtypeStruct((rows, MODEL_WIDTH), BF16)
    return pl.pallas_call(
        functools.partial(attention_backward_kernel, n, slots, group),
        out_shape=(
            jax.ShapeDtypeStruct((rows, MODEL_WIDTH), F32),
            block,
            block,
            block,
            jax.ShapeDtypeStruct((32, MODEL_WIDTH), F32),
        ),
        in_specs=[SMEM] + [ANY] * (4 + n) + [VMEM] * 10,
        out_specs=[VMEM] * 5,
        scratch_shapes=[
            pltpu.VMEM((group, MODEL_WIDTH), BF16),
            pltpu.VMEM((4, MODEL_WIDTH, SET_COLS), BF16),
            pltpu.VMEM((2 * rows, MODEL_WIDTH), BF16),
            pltpu.VMEM((2 * rows, SET_COLS), BF16),
            pltpu.VMEM((SET_HEADS, rows, 128), BF16),
            pltpu.VMEM((SET_HEADS, rows, 128), BF16),
            pltpu.VMEM((group // KEY_BLOCK, SET_COLS, KEY_BLOCK), BF16),
            pltpu.VMEM((group, SET_COLS), F32),
            pltpu.VMEM((group, SET_COLS), F32),
            pltpu.VMEM((SET_COLS, rows), F32),
            pltpu.VMEM((group, 128), BF16),
            pltpu.VMEM((128, MODEL_WIDTH), F32),
            pltpu.VMEM((2, 128, SET_COLS), F32),
            pltpu.SemaphoreType.DMA((4,)),
            pltpu.SemaphoreType.DMA((4,)),
        ],
        compiler_params=pltpu.CompilerParams(vmem_limit_bytes=VMEM_LIMIT),
        cost_estimate=estimate(10_000_000_000, 8_000_000),
        name="attention_backward",
    )(meta, *xs, *pieces, g_low, g_sib, g_own, *saved, adapter, up)


def norm_parts(v):
    mean = jnp.mean(v, axis=-1, keepdims=True)
    centered = v - mean
    rstd = lax.rsqrt(jnp.mean(centered * centered, axis=-1, keepdims=True) + EPSILON)
    return centered * rstd, rstd


def norm_back(g, gain, n, rstd):
    q = g * gain
    return rstd * (
        q - jnp.mean(q, axis=-1, keepdims=True) - n * jnp.mean(q * n, axis=-1, keepdims=True)
    )


def normal_cdf(u):
    z = jnp.abs(u) * 0.7071067811865476
    s = 1.0 / (1.0 + 0.3275911 * z)
    poly = s * (
        0.254829592
        + s * (-0.284496736 + s * (1.421413741 + s * (-1.453152027 + s * 1.061405429)))
    )
    e = jnp.exp(-z * z)
    tail = 0.5 * poly * e
    return jnp.where(u >= 0.0, 1.0 - tail, tail), e * 0.3989422804014327


def split_refs(refs, counts):
    out = []
    for n in counts:
        out.append(refs[:n])
        refs = refs[n:]
    return out, refs


def start_weights(groups, w, sem, shard):
    copies = [
        piece_copies(pieces, lambda p: p, lambda r, m=m: w.at[m, r], sem.at[m], shard)
        for m, pieces in enumerate(groups)
    ]
    for group in copies:
        for c in group:
            c.start()
    return copies


def feedforward_forward_kernel(counts, slots, meta, *refs):
    x, own, sib, vecs, ff_bias = refs[:5]
    groups, refs = split_refs(refs[5:], counts)
    f1_out, f2_out, slope_out, z_out, w, hid, y_scr, sem = refs
    copies = start_weights(groups, w, sem, meta[slots + 1])
    f1 = x[...].astype(F32) + own[...] + sib[...].astype(F32) + vecs[0:1]
    f1_out[...] = f1
    n, _ = norm_parts(f1)
    y = n * vecs[4:5] + vecs[1:2]
    y_scr[...] = y
    y_low = y.astype(BF16)
    rows = x.shape[0]
    for j in range(4):
        for c in copies[2 * j]:
            c.wait()
        for part in range(3):
            cols = slice(part * 256, (part + 1) * 256)
            u = dot_nn(y_low, w[2 * j, :, cols]) + ff_bias[j : j + 1, cols]
            cdf, density = normal_cdf(u)
            hid[j, :, cols] = (u * cdf).astype(BF16)
            slope_out[j, :, cols] = (cdf + u * density).astype(BF16)
    f2 = y_scr[...] + vecs[2:3]
    for j in range(4):
        for c in copies[2 * j + 1]:
            c.wait()
        f2 = f2 + dot_nn(hid[j], w[2 * j + 1])
    f2_out[...] = f2
    n2, _ = norm_parts(f2)
    z_out[...] = (n2 * vecs[5:6] + vecs[3:4]).astype(BF16)


def feedforward_forward(meta, x, own, sib, vecs, ff_bias, groups):
    rows = x.shape[0]
    slots = meta.shape[0] - 2
    counts = [len(g) for g in groups]
    flat = [p for g in groups for p in g]
    wide = jax.ShapeDtypeStruct((rows, MODEL_WIDTH), F32)
    return pl.pallas_call(
        functools.partial(feedforward_forward_kernel, counts, slots),
        out_shape=(
            wide,
            wide,
            jax.ShapeDtypeStruct((4, rows, MODEL_WIDTH), BF16),
            jax.ShapeDtypeStruct((rows, MODEL_WIDTH), BF16),
        ),
        in_specs=[SMEM] + [VMEM] * 5 + [ANY] * len(flat),
        out_specs=[VMEM] * 4,
        scratch_shapes=[
            pltpu.VMEM((8, MODEL_WIDTH, MODEL_WIDTH), BF16),
            pltpu.VMEM((4, rows, MODEL_WIDTH), BF16),
            pltpu.VMEM((rows, MODEL_WIDTH), F32),
            pltpu.SemaphoreType.DMA((8,)),
        ],
        compiler_params=pltpu.CompilerParams(vmem_limit_bytes=VMEM_LIMIT),
        cost_estimate=estimate(6_000_000_000, 12_000_000),
        name="feedforward_forward",
    )(meta, x, own, sib, vecs, ff_bias, *flat)


def feedforward_backward_kernel(counts, slots, n_g, meta, *refs):
    g_refs = refs[:n_g]
    f1, f2, slope, vecs = refs[n_g : n_g + 4]
    groups, refs = split_refs(refs[n_g + 4 :], counts)
    g_out, low_out, w, gu, sem = refs
    copies = start_weights(groups, w, sem, meta[slots + 1])
    g = g_refs[0][...].astype(F32)
    for r in g_refs[1:]:
        g = g + r[...].astype(F32)
    n2, r2 = norm_parts(f2[...])
    gf2 = norm_back(g, vecs[5:6], n2, r2)
    g_out[...] = gf2
    gf2_low = gf2.astype(BF16)
    for j in range(4):
        for c in copies[2 * j + 1]:
            c.wait()
        for part in range(3):
            cols = slice(part * 256, (part + 1) * 256)
            gh = dot_nt(gf2_low, w[2 * j + 1, cols, :])
            gu[j, :, cols] = (gh * slope[j, :, cols].astype(F32)).astype(BF16)
    gy = g_out[...]
    for j in range(4):
        for c in copies[2 * j]:
            c.wait()
        gy = gy + dot_nt(gu[j], w[2 * j])
    n1, r1 = norm_parts(f1[...])
    gf1 = norm_back(gy, vecs[4:5], n1, r1)
    g_out[...] = gf1
    low_out[...] = gf1.astype(BF16)


def feedforward_backward(meta, gs, f1, f2, slope, vecs, groups):
    rows = f1.shape[0]
    slots = meta.shape[0] - 2
    counts = [len(g) for g in groups]
    flat = [p for g in groups for p in g]
    return pl.pallas_call(
        functools.partial(feedforward_backward_kernel, counts, slots, len(gs)),
        out_shape=(
            jax.ShapeDtypeStruct((rows, MODEL_WIDTH), F32),
            jax.ShapeDtypeStruct((rows, MODEL_WIDTH), BF16),
        ),
        in_specs=[SMEM] + [VMEM] * (len(gs) + 4) + [ANY] * len(flat),
        out_specs=[VMEM] * 2,
        scratch_shapes=[
            pltpu.VMEM((8, MODEL_WIDTH, MODEL_WIDTH), BF16),
            pltpu.VMEM((4, rows, MODEL_WIDTH), BF16),
            pltpu.SemaphoreType.DMA((8,)),
        ],
        compiler_params=pltpu.CompilerParams(vmem_limit_bytes=VMEM_LIMIT),
        cost_estimate=estimate(6_000_000_000, 12_000_000),
        name="feedforward_backward",
    )(meta, *gs, f1, f2, slope, vecs, *flat)


def swap(value, axis, flip):
    size = lax.axis_size(axis)
    return lax.ppermute(value, axis, [(i, i ^ flip) for i in range(size)])


def gather_pieces(piece):
    size = lax.axis_size("dp")
    got = {0: piece}
    got[1] = swap(piece, "dp", 1)
    for k in range(2, size, 2):
        got[k] = swap(piece, "dp", k)
    for k in range(2, size, 2):
        got[k + 1] = swap(got[k], "dp", 1)
    return [got[k] for k in range(size)]


def sum_all(value):
    for axis in ("tensor", "dp"):
        size = lax.axis_size(axis)
        flip = 1
        while flip < size:
            value = value + swap(value, axis, flip)
            flip *= 2
    return value


def set_columns(value):
    def part(device, first, last):
        return value[..., device * 192 + first : device * 192 + last]

    return [
        jnp.concatenate(
            [part(s, 0, 128), part(s + 2, 0, 128), part(s, 128, 192), part(s + 2, 128, 192)], -1
        )
        for s in range(2)
    ]


def whole_columns(sets):
    devices = [None] * 4
    for s in range(2):
        v = sets[s]
        devices[s] = jnp.concatenate([v[..., 0:128], v[..., 256:320]], -1)
        devices[s + 2] = jnp.concatenate([v[..., 128:256], v[..., 320:384]], -1)
    return jnp.concatenate(devices, -1)


def body(
    tokens,
    final_output_gradient,
    lengths,
    query_key_value_weight,
    output_projection_weight,
    biases,
    frozen_norm_gains,
    feedforward_in_weight,
    feedforward_bias,
    feedforward_out_weight,
    adapter_down_weights,
    adapter_up_weights,
):
    dp_size = lax.axis_size("dp")
    t = lax.axis_index("tensor")
    shard = lax.axis_index("dp")
    core = t & 1
    upper = t >> 1
    piece_rows = MODEL_WIDTH // dp_size
    pieces_fit = piece_rows % 16 == 0 and dp_size & (dp_size - 1) == 0

    meta = jnp.concatenate(
        [jnp.cumsum(lengths[0]), jnp.stack([t, shard]).astype(jnp.int32)]
    ).astype(jnp.int32)

    def of_core(value):
        first, second = set_columns(value)
        return jnp.where(core == 0, first, second)

    up = of_core(adapter_up_weights.astype(F32) * 2.0).astype(BF16)
    up_pad = [
        jnp.stack(
            [
                jnp.pad(up[l, 0], ((0, 120), (0, 0))),
                jnp.pad(up[l, 1], ((8, 112), (0, 0))),
            ]
        )
        for l in range(ENCODER_LAYERS)
    ]
    head_bias = of_core(biases[:, 0:2])
    adapter = [
        jnp.pad(
            jnp.concatenate([adapter_down_weights[l, 0], adapter_down_weights[l, 1]], -1),
            ((0, 0), (0, 112)),
        )
        for l in range(ENCODER_LAYERS)
    ]
    vecs = [
        jnp.concatenate([biases[l, 2:6], frozen_norm_gains[l], jnp.zeros((2, MODEL_WIDTH), F32)])
        for l in range(ENCODER_LAYERS)
    ]

    def attention_weights(l):
        own = jnp.concatenate([query_key_value_weight[l], output_projection_weight[l][None]])
        other = swap(own, "tensor", 2)
        first = jnp.where(upper == 0, own, other)
        second = jnp.where(upper == 0, other, own)
        piece = jnp.concatenate(
            [first[..., :128], second[..., :128], first[..., 128:], second[..., 128:]], -1
        )
        if pieces_fit:
            return gather_pieces(piece)
        return [lax.all_gather(piece, "dp", axis=1, tiled=True)]

    def direct(own):
        sib = swap(own, "tensor", 1)
        other = swap(own, "tensor", 2)
        return [[own], [sib], [other], [swap(other, "tensor", 1)]]

    def ringed(own):
        sib = swap(own, "tensor", 1)
        piece = swap(
            lax.dynamic_slice_in_dim(own, shard * piece_rows, piece_rows, 0), "tensor", 2
        )
        pieces = gather_pieces(piece)
        return [[own], [sib], pieces, [swap(p, "tensor", 1) for p in pieces]]

    def feedforward_weights(l, ring_in, ring_out):
        parts = []
        for value, ring in (
            (feedforward_in_weight[l], ring_in),
            (feedforward_out_weight[l], ring_out),
        ):
            parts.append(ringed(value) if ring and pieces_fit else direct(value))
        return [parts[m][j] for j in range(4) for m in range(2)]

    def gather_rows(rows):
        other = swap(rows, "tensor", 2)
        return [rows, swap(rows, "tensor", 1), other, swap(other, "tensor", 1)]

    att_w = [attention_weights(0)]
    bias_rows = jnp.pad(feedforward_bias, ((0, 14), (0, 0)))
    first_rows = gather_rows(jnp.concatenate([tokens, bias_rows]))
    n_rows = tokens.shape[0]
    x = [[r[:n_rows] for r in first_rows]]
    ff_bias = [
        jnp.stack([r[n_rows + l] for r in first_rows]).astype(F32) for l in range(ENCODER_LAYERS)
    ]
    ff_w = [feedforward_weights(0, False, True)]
    att_w.append(attention_weights(1))
    ff_w.append(feedforward_weights(1, True, True))

    saved = []
    rows = tokens
    for l in range(ENCODER_LAYERS):
        if l > 0:
            x.append(gather_rows(rows))
        q, k, v, lse, c, own, sib = attention_forward(
            meta, x[l], att_w[l], adapter[l], up_pad[l], head_bias[l]
        )
        sib = swap(sib, "tensor", 1)
        f1, f2, slope, rows = feedforward_forward(
            meta, rows, own, sib, vecs[l], ff_bias[l], ff_w[l]
        )
        saved.append((q, k, v, lse, c, f1, f2, slope))

    gs = [final_output_gradient]
    small = [None] * ENCODER_LAYERS
    for l in reversed(range(ENCODER_LAYERS)):
        q, k, v, lse, c, f1, f2, slope = saved[l]
        g_first, g_low = feedforward_backward(meta, gs, f1, f2, slope, vecs[l], ff_w[l])
        p0, p1, p2, p3, grads = attention_backward(
            meta,
            x[l],
            att_w[l],
            g_low,
            swap(g_low, "tensor", 1),
            g_first,
            (q, k, v, lse, c),
            adapter[l],
            up_pad[l],
        )
        p3 = swap(p3, "tensor", 1)
        p1 = swap(p1, "tensor", 1)
        p2 = swap((p2.astype(F32) + p3.astype(F32)).astype(BF16), "tensor", 2)
        gs = [p0, p1, p2]
        small[l] = sum_all(grads)

    input_grad = sum(g.astype(F32) for g in gs).astype(BF16)
    both = jnp.stack(small)
    shape = (ENCODER_LAYERS, 2, ADAPTER_RANK, MODEL_WIDTH)
    grad_a = both[:, :16].reshape(shape).swapaxes(2, 3)
    grad_b = both[:, 16:].reshape(shape)
    grad_b = whole_columns([grad_b[..., :SET_COLS], grad_b[..., SET_COLS:]])
    return rows, input_grad, grad_a, grad_b


def solution(mesh):
    return jax.shard_map(
        body,
        mesh=mesh,
        in_specs=(
            P(("dp", "tensor"), None),
            P(("dp", "tensor"), None),
            P("dp", None),
            P(None, None, "dp", "tensor"),
            P(None, "dp", "tensor"),
            P(),
            P(),
            P(None, None, "tensor"),
            P(None, "tensor"),
            P(None, "tensor", None),
            P(),
            P(),
        ),
        out_specs=(P(("dp", "tensor"), None), P(("dp", "tensor"), None), P(), P()),
        check_vma=False,
    )
```

```python
from types import SimpleNamespace

import jax
import jax.numpy as jnp
from jax import lax
from jax.experimental import pallas as pl
from jax.experimental.pallas import tpu as pltpu
from jax.sharding import PartitionSpec as P

MODEL_WIDTH = 768
HEAD_DIM = 64
ADAPTER_RANK = 8
ENCODER_LAYERS = 2
HEADS = 12
SET_COLS = 384
HEAD_GROUP = 6
KEY_BLOCK = 128
EPSILON = 1e-05
MASKED = -1000000000.0
VMEM_LIMIT = 56 * 1024 * 1024

F32 = jnp.float32
BF16 = jnp.bfloat16
ANY = pl.ANY
VMEM = pltpu.VMEM
SMEM = pltpu.SMEM


def dot_nn(a, b):
    return lax.dot_general(a, b, (((1,), (0,)), ((), ())), preferred_element_type=F32)


def dot_nt(a, b):
    return lax.dot_general(a, b, (((1,), (1,)), ((), ())), preferred_element_type=F32)


def dot_tn(a, b):
    return lax.dot_general(a, b, (((0,), (0,)), ((), ())), preferred_element_type=F32)


def aligned(start, size):
    return pl.ds(pl.multiple_of(start, size), size)


def run_kernel(name, kernel, inputs, outputs, scratch, flops, nbytes, spaces={}):
    flat, specs, layout = [], [], []
    for key, (space, value) in inputs.items():
        many = isinstance(value, list)
        values = value if many else [value]
        layout.append((key, len(values), many))
        flat += values
        specs += [pl.BlockSpec(memory_space=space)] * len(values)

    def whole(*refs):
        named, at = {}, 0
        for key, count, many in layout:
            named[key] = list(refs[at : at + count]) if many else refs[at]
            at += count
        for key in (*outputs, *scratch):
            named[key] = refs[at]
            at += 1
        kernel(SimpleNamespace(**named))

    result = pl.pallas_call(
        whole,
        out_shape=tuple(outputs.values()),
        in_specs=specs,
        out_specs=tuple(pl.BlockSpec(memory_space=spaces.get(k, VMEM)) for k in outputs),
        scratch_shapes=list(scratch.values()),
        compiler_params=pltpu.CompilerParams(vmem_limit_bytes=VMEM_LIMIT),
        cost_estimate=pl.CostEstimate(flops=flops, bytes_accessed=nbytes, transcendentals=0),
        name=name,
    )(*flat)
    return dict(zip(outputs, result))


class Queue:
    def __init__(self, ahead):
        self.ahead, self.groups, self.started = ahead, [], 0

    def add(self, copies):
        self.groups.append(copies)
        return len(self.groups) - 1

    def start_to(self, last):
        while self.started < min(last, len(self.groups)):
            for c in self.groups[self.started]:
                c.start()
            self.started += 1

    def wait(self, at):
        self.start_to(at + 1 + self.ahead)
        for c in self.groups[at]:
            c.wait()
        self.groups[at] = []


def piece_copies(pieces, source_of, target_of, sem, meta):
    out = []
    rows = MODEL_WIDTH // len(pieces)
    for k, piece in enumerate(pieces):
        if len(pieces) == 1:
            target = target_of(pl.ds(0, rows))
        else:
            target = target_of(aligned(meta[4 + k] * rows, rows))
        out.append(pltpu.make_async_copy(source_of(piece), target, sem))
    return out


def meta_of(r):
    return r.meta[0], r.meta[2], r.meta[3]


def attention_weight_copies(r):
    core = jnp.bitwise_and(r.meta[0], 1)
    out = []
    for m in range(4):
        copies = []
        for pieces, s in ((r.att_own, core), (r.att_sib, 1 - core)):
            copies += piece_copies(
                pieces,
                lambda p, m=m: p.at[m],
                lambda rows, m=m, s=s: r.w.at[m, s, rows],
                r.w_sem.at[m],
                r.meta,
            )
        out.append(copies)
    return out


def feedforward_weight_copies(r, layer):
    whole = (r.in_own.at[layer], r.out_own.at[layer], r.in_sib.at[layer], r.out_sib.at[layer])
    out = [[pltpu.make_async_copy(v, r.ff.at[m], r.ff_sem.at[m])] for m, v in enumerate(whole)]
    for m, value, far, pieces in (
        (4, r.in_far, r.out_far, r.att_own),
        (6, r.in_far_sib, r.out_far_sib, r.att_sib),
    ):
        copies, at = [], 0
        for part in value:
            rows = pl.ds(at, part.shape[0])
            copies.append(pltpu.make_async_copy(part, r.ff.at[m, rows], r.ff_sem.at[m]))
            at += part.shape[0]
        out.append(copies)
        if far:
            out.append([pltpu.make_async_copy(far[0], r.ff.at[m + 1], r.ff_sem.at[m + 1])])
            continue
        copies = []
        for half in range(2):
            cols = pl.ds(half * SET_COLS, SET_COLS)
            copies += piece_copies(
                pieces,
                lambda p, half=half: p.at[4 + half],
                lambda rows, m=m, cols=cols: r.ff.at[m + 1, rows, cols],
                r.ff_sem.at[m + 1],
                r.meta,
            )
        out.append(copies)
    return out


def bias_copies(r):
    rows = r.ends.shape[1]
    return [
        pltpu.make_async_copy(first.at[pl.ds(rows, 16)], r.bias_rows.at[j], r.bias_sem)
        for j, first in enumerate(r.first_rows)
    ]


def row_copies(r):
    t = r.meta[0]
    rows = r.ends.shape[1]
    return [
        pltpu.make_async_copy(
            r.rows[j].at[pl.ds(0, rows)], r.xs.at[aligned(jnp.bitwise_xor(t, j) * rows, rows)], r.x_sem.at[j]
        )
        for j in range(4)
    ]


def pair_cols(h):
    return slice((h // 2) * 128, (h // 2 + 1) * 128)


def head_cols(h):
    return slice(h * HEAD_DIM, (h + 1) * HEAD_DIM)


def keep_head(value, h):
    lane = lax.broadcasted_iota(jnp.int32, value.shape, 1)
    keep = (lane < HEAD_DIM) if h % 2 == 0 else (lane >= HEAD_DIM)
    return jnp.where(keep, value, jnp.zeros_like(value))


def key_mask(r, kb, rows):
    kpos = kb * KEY_BLOCK + lax.broadcasted_iota(jnp.int32, (KEY_BLOCK, rows), 0)
    return jnp.where((kpos >= r.ends[0:1]) & (kpos < r.ends[1:2]), 0.0, MASKED)


def attention_forward_stage(r, queue, rows_at, weights_at):
    t, low, high = meta_of(r)
    rows_dev = r.ends.shape[1]
    per = rows_dev // KEY_BLOCK
    own = aligned(t * rows_dev, rows_dev)
    for at in (rows_at, weights_at[1], weights_at[2]):
        queue.wait(at)

    def project_block(b, _):
        rows = aligned(b * rows_dev, rows_dev)
        xb = r.xs[rows]
        db = dot_nn(xb, r.adapter[...]).astype(BF16)
        r.down[rows] = db
        for s in range(2):
            cols = slice(s * SET_COLS, (s + 1) * SET_COLS)
            kb = dot_nn(xb, r.w[1, s]).astype(BF16)
            r.k[rows, cols] = kb
            kb_t = kb.T
            vb = (dot_nn(xb, r.w[2, s]) + dot_nn(db, r.up[1, :, cols]) + r.vecs[7:8, cols]).astype(BF16)
            r.v[rows, cols] = vb
            vb_t = vb.T
            for i in range(per):
                keys = slice(i * KEY_BLOCK, (i + 1) * KEY_BLOCK)
                r.kt[b * per + i, cols, :] = kb_t[:, keys]
                r.vt[b * per + i, cols, :] = vb_t[:, keys]
        return 0

    lax.fori_loop(low // rows_dev, (high + rows_dev - 1) // rows_dev, project_block, 0)

    queue.wait(weights_at[0])
    for s in range(2):
        cols = slice(s * SET_COLS, (s + 1) * SET_COLS)
        qv = dot_nn(r.xs[own], r.w[0, s]) + dot_nn(r.down[own], r.up[0, :, cols]) + r.vecs[6:7, cols]
        r.q[:, cols] = (qv * HEAD_DIM**-0.5).astype(BF16)
    for h in range(HEADS):
        r.qm[h] = keep_head(r.q[:, pair_cols(h)], h)
    r.acc[...] = jnp.zeros_like(r.acc)
    r.tops[...] = jnp.full_like(r.tops, -3e38)
    r.sums[...] = jnp.zeros_like(r.sums)

    def key_step(kb, _):
        keys = aligned(kb * KEY_BLOCK, KEY_BLOCK)
        mask = key_mask(r, kb, rows_dev)
        for first in range(0, HEADS, HEAD_GROUP):
            heads = range(first, first + HEAD_GROUP)
            s = [dot_nt(r.k[keys, pair_cols(h)], r.qm[h]) + mask for h in heads]
            old = [r.tops[h : h + 1] for h in heads]
            top = [jnp.maximum(o, jnp.max(v, axis=0, keepdims=True)) for o, v in zip(old, s)]
            fade = [jnp.exp(o - n) for o, n in zip(old, top)]
            p = [jnp.exp(v - n) for v, n in zip(s, top)]
            low_p = [v.astype(BF16) for v in p]
            for i, h in enumerate(heads):
                r.tops[h : h + 1] = top[i]
                r.sums[h : h + 1] = r.sums[h : h + 1] * fade[i] + jnp.sum(p[i], axis=0, keepdims=True)
            for i, h in enumerate(heads):
                cols = head_cols(h)
                r.acc[cols] = r.acc[cols] * fade[i] + dot_nn(r.vt[kb, cols, :], low_p[i])
        return 0

    lax.fori_loop(low // KEY_BLOCK, (high + KEY_BLOCK - 1) // KEY_BLOCK, key_step, 0)
    for h in range(HEADS):
        r.acc[head_cols(h)] = r.acc[head_cols(h)] / r.sums[h : h + 1]
    r.lse[...] = r.tops[...] + jnp.log(r.sums[...])
    r.c[...] = r.acc[...].T.astype(BF16)
    queue.wait(weights_at[3])
    f1 = r.xs[own].astype(F32) + r.vecs[0:1]
    for s in range(2):
        f1 = f1 + dot_nt(r.c[:, s * SET_COLS : (s + 1) * SET_COLS], r.w[3, s])
    r.f1[...] = f1


def struct(shape, dtype):
    return jax.ShapeDtypeStruct(shape, dtype)


def attention_inputs(x, weights, small):
    own, sib = weights
    return {
        "meta": (SMEM, small["meta"]),
        "ends": (VMEM, small["ends"]),
        "adapter": (VMEM, small["adapter"]),
        "up": (VMEM, small["up"]),
        "vecs": (VMEM, small["vecs"]),
        "rows": (ANY, x),
        "att_own": (ANY, own),
        "att_sib": (ANY, sib),
    }


def attention_scratch(rows):
    return {
        "xs": VMEM((4 * rows, MODEL_WIDTH), BF16),
        "w": VMEM((4, 2, MODEL_WIDTH, SET_COLS), BF16),
        "qm": VMEM((HEADS, rows, 128), BF16),
        "acc": VMEM((MODEL_WIDTH, rows), F32),
        "x_sem": pltpu.SemaphoreType.DMA((4,)),
        "w_sem": pltpu.SemaphoreType.DMA((4,)),
    }


def attention_forward(x, weights, small):
    rows = small["ends"].shape[1]
    group = 4 * rows
    blocks = group // KEY_BLOCK

    def kernel(r):
        queue = Queue(2)
        rows_at = queue.add(row_copies(r))
        copies = attention_weight_copies(r)
        weights_at = {m: queue.add(copies[m]) for m in (1, 2, 0, 3)}
        attention_forward_stage(r, queue, rows_at, weights_at)

    return run_kernel(
        "attention_forward",
        kernel,
        attention_inputs(x, weights, small),
        {
            "q": struct((rows, MODEL_WIDTH), BF16),
            "k": struct((group, MODEL_WIDTH), BF16),
            "v": struct((group, MODEL_WIDTH), BF16),
            "kt": struct((blocks, MODEL_WIDTH, KEY_BLOCK), BF16),
            "down": struct((group, 128), BF16),
            "lse": struct((16, rows), F32),
            "c": struct((rows, MODEL_WIDTH), BF16),
            "f1": struct((rows, MODEL_WIDTH), F32),
        },
        {
            **attention_scratch(rows),
            "vt": VMEM((blocks, MODEL_WIDTH, KEY_BLOCK), BF16),
            "tops": VMEM((16, rows), F32),
            "sums": VMEM((16, rows), F32),
        },
        8_000_000_000,
        12_000_000,
    )


def attention_backward_stage(r, queue, rows_at, state_at, weights_at):
    t, low, high = meta_of(r)
    rows_dev = r.ends.shape[1]
    block_low = low // rows_dev
    block_high = (high + rows_dev - 1) // rows_dev

    def clear_block(b, _):
        rows = aligned(b * rows_dev, rows_dev)
        r.gk[rows] = jnp.zeros((rows_dev, MODEL_WIDTH), F32)
        r.gv[rows] = jnp.zeros((rows_dev, MODEL_WIDTH), F32)
        return 0

    lax.fori_loop(block_low, block_high, clear_block, 0)
    r.acc[...] = jnp.zeros_like(r.acc)
    queue.wait(weights_at[3])
    gf1_low = r.gf1[...].astype(BF16)
    for s in range(2):
        r.gc[:, s * SET_COLS : (s + 1) * SET_COLS] = dot_nn(gf1_low, r.w[3, s]).astype(BF16)
    queue.wait(state_at)
    pick = (
        lax.broadcasted_iota(jnp.int32, (16, MODEL_WIDTH), 1) // HEAD_DIM
        == lax.broadcasted_iota(jnp.int32, (16, MODEL_WIDTH), 0)
    ).astype(BF16)
    product = r.gc[...].astype(F32) * r.c[...].astype(F32)
    product_high = product.astype(BF16)
    product_low = (product - product_high.astype(F32)).astype(BF16)
    r.delta[...] = dot_nt(pick, product_high) + dot_nt(pick, product_low)
    for h in range(HEADS):
        r.qm[h] = keep_head(r.q[:, pair_cols(h)], h)
        r.gcm[h] = keep_head(r.gc[:, pair_cols(h)], h)

    def key_step(kb, _):
        keys = aligned(kb * KEY_BLOCK, KEY_BLOCK)
        mask = key_mask(r, kb, rows_dev)
        for first in range(0, HEADS, HEAD_GROUP):
            heads = range(first, first + HEAD_GROUP)
            s = [dot_nt(r.k[keys, pair_cols(h)], r.qm[h]) + mask for h in heads]
            gp = [dot_nt(r.v[keys, pair_cols(h)], r.gcm[h]) for h in heads]
            p = [jnp.exp(v - r.lse[h : h + 1]) for h, v in zip(heads, s)]
            gs = [
                (pv * (gv - r.delta[h : h + 1])).astype(BF16) for h, pv, gv in zip(heads, p, gp)
            ]
            low_p = [v.astype(BF16) for v in p]
            for i, h in enumerate(heads):
                r.acc[head_cols(h)] += dot_nn(r.kt[kb, head_cols(h), :], gs[i])
            for i in range(0, HEAD_GROUP, 2):
                h = first + i
                cols = pair_cols(h)
                r.gk[keys, cols] += dot_nn(gs[i], r.qm[h]) + dot_nn(gs[i + 1], r.qm[h + 1])
                r.gv[keys, cols] += dot_nn(low_p[i], r.gcm[h]) + dot_nn(low_p[i + 1], r.gcm[h + 1])
        return 0

    lax.fori_loop(low // KEY_BLOCK, (high + KEY_BLOCK - 1) // KEY_BLOCK, key_step, 0)
    r.gc[...] = (r.acc[...].T * HEAD_DIM**-0.5).astype(BF16)

    for at in (rows_at, weights_at[0], weights_at[1], weights_at[2]):
        queue.wait(at)
    r.ga[...] = jnp.zeros_like(r.ga)
    r.gb[...] = jnp.zeros_like(r.gb)

    def key_value_gradient(b):
        rows = aligned(b * rows_dev, rows_dev)
        gkb = r.gk[rows].astype(BF16)
        gvb = r.gv[rows].astype(BF16)
        g = None
        for s in range(2):
            cols = slice(s * SET_COLS, (s + 1) * SET_COLS)
            term = dot_nt(gkb[:, cols], r.w[1, s]) + dot_nt(gvb[:, cols], r.w[2, s])
            g = term if g is None else g + term
        r.gb[1] += dot_tn(r.down[rows], gvb)
        return g, dot_nt(gvb, r.up[1])

    def add_adapter(b, g, gd):
        gd = gd.astype(BF16)
        r.ga[...] += dot_tn(gd, r.xs[aligned(b * rows_dev, rows_dev)])
        return g + dot_nt(gd, r.adapter[...])

    for j, out in ((2, r.p2), (3, r.p3), (1, r.p1)):
        b = jnp.bitwise_xor(t, j)
        used = (b >= block_low) & (b < block_high)

        @pl.when(used)
        def _(b=b, out=out):
            g, gd = key_value_gradient(b)
            out[...] = add_adapter(b, g, gd).astype(BF16)

        @pl.when(jnp.logical_not(used))
        def _(out=out):
            out[...] = jnp.zeros_like(out)

    g, gd = key_value_gradient(t)
    gq = r.gc[...]
    for s in range(2):
        g = g + dot_nt(gq[:, s * SET_COLS : (s + 1) * SET_COLS], r.w[0, s])
    gd = gd + dot_nt(gq, r.up[0])
    r.gb[0] += dot_tn(r.down[aligned(t * rows_dev, rows_dev)], gq)
    r.p0[...] = add_adapter(t, g, gd) + r.gf1[...]
    r.grads[0:16] = r.ga[0:16]
    r.grads[16:24] = r.gb[0, 0:8] * 2.0
    r.grads[24:32] = r.gb[1, 8:16] * 2.0


def norm_parts(v):
    mean = jnp.mean(v, axis=-1, keepdims=True)
    centered = v - mean
    rstd = lax.rsqrt(jnp.mean(centered * centered, axis=-1, keepdims=True) + EPSILON)
    return centered * rstd, rstd


def norm_back(g, gain, n, rstd):
    q = g * gain
    return rstd * (
        q - jnp.mean(q, axis=-1, keepdims=True) - n * jnp.mean(q * n, axis=-1, keepdims=True)
    )


def normal_cdf(u):
    z = jnp.abs(u) * 0.7071067811865476
    s = 1.0 / (1.0 + 0.3275911 * z)
    poly = s * (
        0.254829592
        + s * (-0.284496736 + s * (1.421413741 + s * (-1.453152027 + s * 1.061405429)))
    )
    e = jnp.exp(-z * z)
    tail = 0.5 * poly * e
    return jnp.where(u >= 0.0, 1.0 - tail, tail), e * 0.3989422804014327


def feedforward_forward_stage(r, queue, bias_at, weights_at, layer):
    n, _ = norm_parts(r.f1[...])
    y = n * r.vecs[4:5] + r.vecs[1:2]
    r.f2[...] = y + r.vecs[2:3]
    y_low = y.astype(BF16)
    queue.wait(bias_at)
    for j in range(4):
        r.ff_bias[j : j + 1] = r.bias_rows[j].astype(F32)[layer : layer + 1]
    for j in range(4):
        queue.wait(weights_at[2 * j])
        for part in range(3):
            cols = slice(part * 256, (part + 1) * 256)
            u = dot_nn(y_low, r.ff[2 * j, :, cols]) + r.ff_bias[j : j + 1, cols]
            cdf, density = normal_cdf(u)
            r.hid[j, :, cols] = (u * cdf).astype(BF16)
            r.slope[j, :, cols] = (cdf + u * density).astype(BF16)
    f2 = r.f2[...]
    for j in range(4):
        queue.wait(weights_at[2 * j + 1])
        f2 = f2 + dot_nn(r.hid[j], r.ff[2 * j + 1])
    r.f2[...] = f2
    n2, _ = norm_parts(f2)
    r.z[...] = (n2 * r.vecs[5:6] + r.vecs[3:4]).astype(BF16)


def feedforward_backward_stage(r, queue, weights_at):
    g = r.gs[0][...].astype(F32)
    for part in r.gs[1:]:
        g = g + part[...].astype(F32)
    n2, r2 = norm_parts(r.f2[...])
    gf2 = norm_back(g, r.vecs[5:6], n2, r2)
    r.gf1[...] = gf2
    gf2_low = gf2.astype(BF16)
    for j in range(4):
        queue.wait(weights_at[2 * j + 1])
        for part in range(3):
            cols = slice(part * 256, (part + 1) * 256)
            gh = dot_nt(gf2_low, r.ff[2 * j + 1, cols, :])
            r.hid[j, :, cols] = (gh * r.slope[j, :, cols].astype(F32)).astype(BF16)
    gy = r.gf1[...]
    for j in range(4):
        queue.wait(weights_at[2 * j])
        gy = gy + dot_nt(r.hid[j], r.ff[2 * j])
    n1, r1 = norm_parts(r.f1[...])
    r.gf1[...] = norm_back(gy, r.vecs[4:5], n1, r1)


def feedforward_scratch(rows):
    return {
        "ff": VMEM((8, MODEL_WIDTH, MODEL_WIDTH), BF16),
        "hid": VMEM((4, rows, MODEL_WIDTH), BF16),
        "ff_sem": pltpu.SemaphoreType.DMA((8,)),
        "bias_rows": VMEM((4, 16, MODEL_WIDTH), BF16),
        "ff_bias": VMEM((8, MODEL_WIDTH), F32),
        "bias_sem": pltpu.SemaphoreType.DMA,
    }


def feedforward_inputs(weights):
    names = ("in_own", "out_own", "in_sib", "out_sib", "in_far", "in_far_sib", "out_far", "out_far_sib", "first_rows")
    return {k: (ANY, v) for k, v in zip(names, weights)}


def feedforward_forward(f1, weights, ff_weights, small, layer):
    rows = f1.shape[0]

    def kernel(r):
        queue = Queue(3)
        bias_at = queue.add(bias_copies(r))
        copies = feedforward_weight_copies(r, layer)
        weights_at = {m: queue.add(copies[m]) for m in (0, 2, 4, 6, 1, 3, 5, 7)}
        queue.start_to(4)
        feedforward_forward_stage(r, queue, bias_at, weights_at, layer)

    return run_kernel(
        "feedforward_forward",
        kernel,
        {
            "meta": (SMEM, small["meta"]),
            "vecs": (VMEM, small["vecs"]),
            "ends": (VMEM, small["ends"]),
            "f1": (VMEM, f1),
            "att_own": (ANY, weights[0]),
            "att_sib": (ANY, weights[1]),
            **feedforward_inputs(ff_weights),
        },
        {
            "f2": struct((rows, MODEL_WIDTH), F32),
            "slope": struct((4, rows, MODEL_WIDTH), BF16),
            "z": struct((rows, MODEL_WIDTH), BF16),
        },
        feedforward_scratch(rows),
        6_000_000_000,
        12_000_000,
    )


def layer_backward(gs, x, weights, ff_weights, saved, small, layer, forward):
    rows = small["ends"].shape[1]
    group = 4 * rows
    blocks = group // KEY_BLOCK
    state = {
        "q": VMEM((rows, MODEL_WIDTH), BF16),
        "c": VMEM((rows, MODEL_WIDTH), BF16),
        "lse": VMEM((16, rows), F32),
        "k": VMEM((group, MODEL_WIDTH), BF16),
        "v": VMEM((group, MODEL_WIDTH), BF16),
        "kt": VMEM((blocks, MODEL_WIDTH, KEY_BLOCK), BF16),
        "down": VMEM((group, 128), BF16),
    }
    wide = {"f2": (rows, MODEL_WIDTH, F32), "slope": (4, rows, MODEL_WIDTH, BF16)}

    def kernel(r):
        queue = Queue(3)
        if forward:
            bias_at = queue.add(bias_copies(r))
        copies = feedforward_weight_copies(r, layer)
        order = (0, 2, 4, 6, 1, 3, 5, 7) if forward else (1, 3, 5, 7, 0, 2, 4, 6)
        ff_at = {m: queue.add(copies[m]) for m in order}
        queue.start_to(4)
        copies = attention_weight_copies(r)
        weights_at = {3: queue.add(copies[3])}
        state_at = queue.add(
            [
                pltpu.make_async_copy(getattr(r, "saved_" + k), getattr(r, k), r.state_sem)
                for k in state
            ]
        )
        rows_at = queue.add(row_copies(r))
        weights_at.update({m: queue.add(copies[m]) for m in (0, 1, 2)})
        if forward:
            feedforward_forward_stage(r, queue, bias_at, ff_at, layer)
        feedforward_backward_stage(r, queue, ff_at)
        attention_backward_stage(r, queue, rows_at, state_at, weights_at)

    inputs = attention_inputs(x, weights, small)
    inputs["gs"] = (VMEM, gs)
    inputs["f1"] = (VMEM, saved["f1"])
    inputs.update({"saved_" + k: (ANY, saved[k]) for k in state})
    inputs.update(feedforward_inputs(ff_weights))
    block = struct((rows, MODEL_WIDTH), BF16)
    outputs = {
        "p0": struct((rows, MODEL_WIDTH), F32),
        "p1": block,
        "p2": block,
        "p3": block,
        "grads": struct((32, MODEL_WIDTH), F32),
    }
    scratch = {
        **attention_scratch(rows),
        **feedforward_scratch(rows),
        **state,
        "gf1": VMEM((rows, MODEL_WIDTH), F32),
        "gc": VMEM((rows, MODEL_WIDTH), BF16),
        "gcm": VMEM((HEADS, rows, 128), BF16),
        "delta": VMEM((16, rows), F32),
        "gk": VMEM((group, MODEL_WIDTH), F32),
        "gv": VMEM((group, MODEL_WIDTH), F32),
        "ga": VMEM((128, MODEL_WIDTH), F32),
        "gb": VMEM((2, 128, MODEL_WIDTH), F32),
        "state_sem": pltpu.SemaphoreType.DMA,
    }
    if forward:
        outputs["z"] = block
        scratch["f2"] = VMEM((rows, MODEL_WIDTH), F32)
        scratch["slope"] = VMEM((4, rows, MODEL_WIDTH), BF16)
    else:
        inputs["f2"] = (VMEM, saved["f2"])
        inputs["slope"] = (VMEM, saved["slope"])
    return run_kernel(
        "layer_backward", kernel, inputs, outputs, scratch, 20_000_000_000, 25_000_000
    )


def set_columns(value):
    def part(device, first, last):
        return value[..., device * 192 + first : device * 192 + last]

    out = []
    for s in range(2):
        out += [part(s, 0, 128), part(s + 2, 0, 128), part(s, 128, 192), part(s + 2, 128, 192)]
    return jnp.concatenate(out, -1)


def whole_columns(value):
    devices = [None] * 4
    for s in range(2):
        v = value[..., s * SET_COLS : (s + 1) * SET_COLS]
        devices[s] = jnp.concatenate([v[..., 0:128], v[..., 256:320]], -1)
        devices[s + 2] = jnp.concatenate([v[..., 128:256], v[..., 320:384]], -1)
    return jnp.concatenate(devices, -1)


def prepare(lengths, place, biases, gains, down, up, rows, group, size):
    slots = lengths.shape[1]
    order = ring_order(size)

    def kernel(r):
        t, shard = r.place[0], r.place[1]
        row = t * rows + lax.broadcasted_iota(jnp.int32, (1, rows), 1)
        start = jnp.zeros((1, rows), jnp.int32)
        stop = jnp.full((1, rows), group, jnp.int32)
        low, high, end = jnp.int32(0), jnp.int32(group), jnp.int32(0)
        for s in range(slots):
            end = end + r.lengths[0, s]
            start = jnp.where(end <= row, end, start)
            stop = jnp.where(end > row, jnp.minimum(stop, end), stop)
            low = jnp.where(end <= t * rows, end, low)
            high = jnp.where(end > t * rows + rows - 1, jnp.minimum(high, end), high)
        r.ends[0:1] = start
        r.ends[1:2] = stop
        r.meta[0] = t
        r.meta[1] = shard
        r.meta[2] = low
        r.meta[3] = high

        def device(position):
            out = jnp.int32(0)
            for k, d in enumerate(order):
                out = jnp.where(position == k, d, out)
            return out

        at = jnp.int32(0)
        for k, d in enumerate(order):
            at = jnp.where(shard == d, k, at)
        count = 4
        for step in range(size // 2 + 1):
            r.meta[count] = device(jnp.where(at - step < 0, at - step + size, at - step))
            count += 1
            if 0 < 2 * step < size:
                r.meta[count] = device(jnp.where(at + step >= size, at + step - size, at + step))
                count += 1

        lane = lax.broadcasted_iota(jnp.int32, (ADAPTER_RANK, 128), 1)
        sub = lax.broadcasted_iota(jnp.int32, (ADAPTER_RANK, 128), 0)
        none = jnp.zeros((ADAPTER_RANK, MODEL_WIDTH), F32)
        for l in range(ENCODER_LAYERS):
            both = jnp.zeros((MODEL_WIDTH, 128), F32)
            for m in range(2):
                put = (lane == sub + m * ADAPTER_RANK).astype(BF16)
                both = both + dot_nn(r.down[l, m], put)
            getattr(r, f"adapter{l}")[...] = both.astype(BF16)
            ups = getattr(r, f"up{l}")
            ups[...] = jnp.zeros_like(ups)
            for m in range(2):
                value = set_columns(r.up[l, m].astype(F32)) * 2.0
                value = jnp.concatenate([value, none] if m == 0 else [none, value], 0)
                ups[m, 0:16] = value.astype(BF16)
            vecs = getattr(r, f"vecs{l}")
            vecs[0:4] = r.biases[l, 2:6]
            vecs[4:6] = r.gains[l]
            vecs[6:8] = set_columns(r.biases[l, 0:2])

    outputs = {
        "meta": struct((4 + size,), jnp.int32),
        "ends": struct((2, rows), jnp.int32),
    }
    for l in range(ENCODER_LAYERS):
        outputs[f"adapter{l}"] = struct((MODEL_WIDTH, 128), BF16)
        outputs[f"up{l}"] = struct((2, 128, MODEL_WIDTH), BF16)
        outputs[f"vecs{l}"] = struct((8, MODEL_WIDTH), F32)
    return run_kernel(
        "prepare",
        kernel,
        {
            "lengths": (SMEM, lengths),
            "place": (SMEM, place),
            "biases": (VMEM, biases),
            "gains": (VMEM, gains),
            "down": (VMEM, down),
            "up": (VMEM, up),
        },
        outputs,
        {},
        100_000_000,
        2_000_000,
        {"meta": SMEM},
    )


def finish(sums):
    def kernel(r):
        for l in range(ENCODER_LAYERS):
            for m in range(2):
                at = m * ADAPTER_RANK
                r.grad_a[l, m] = r.sums[l][at : at + ADAPTER_RANK].T
                r.grad_b[l, m] = whole_columns(r.sums[l][16 + at : 16 + at + ADAPTER_RANK])

    out = run_kernel(
        "finish",
        kernel,
        {"sums": (VMEM, sums)},
        {
            "grad_a": struct((ENCODER_LAYERS, 2, MODEL_WIDTH, ADAPTER_RANK), F32),
            "grad_b": struct((ENCODER_LAYERS, 2, ADAPTER_RANK, MODEL_WIDTH), F32),
        },
        {},
        1_000_000,
        1_000_000,
    )
    return out["grad_a"], out["grad_b"]


def swap(value, axis, flip):
    size = lax.axis_size(axis)
    return lax.ppermute(value, axis, [(i, i ^ flip) for i in range(size)])


def ring_order(size):
    return list(range(0, size, 2)) + list(range(1, size, 2))[::-1]


class RingGather:
    def __init__(self, piece):
        self.size = lax.axis_size("dp")
        order = ring_order(self.size)
        self.up = [(order[i], order[(i + 1) % self.size]) for i in range(self.size)]
        self.down = [(b, a) for a, b in self.up]
        self.got, self.sib = [piece], []
        self.going_up = self.going_down = piece
        self.steps = 0

    def left(self):
        return self.steps < self.size // 2

    def step(self, gate=()):
        self.steps += 1
        self.going_up = lax.ppermute(after(self.going_up, *gate), "dp", self.up)
        out = [self.going_up]
        if 2 * self.steps < self.size:
            self.going_down = lax.ppermute(after(self.going_down, *gate), "dp", self.down)
            out.append(self.going_down)
        self.got += out
        return out

    def other_core(self, *gate):
        for value in self.got[len(self.sib) :]:
            self.sib.append(swap(after(value, *gate), "tensor", 1))


def after(value, *others):
    return lax.optimization_barrier((value, *others))[0] if others else value


def sum_all(value):
    for axis in ("tensor", "dp"):
        size = lax.axis_size(axis)
        flip = 1
        while flip < size:
            low = value.astype(BF16)
            value = low.astype(F32) + swap(low, axis, flip).astype(F32)
            flip *= 2
    return value


def body(
    tokens,
    final_output_gradient,
    lengths,
    query_key_value_weight,
    output_projection_weight,
    biases,
    frozen_norm_gains,
    feedforward_in_weight,
    feedforward_bias,
    feedforward_out_weight,
    adapter_down_weights,
    adapter_up_weights,
):
    dp_size = lax.axis_size("dp")
    t = lax.axis_index("tensor")
    shard = lax.axis_index("dp")
    upper = t >> 1
    piece_rows = MODEL_WIDTH // dp_size
    pieces_fit = piece_rows % 16 == 0 and dp_size & (dp_size - 1) == 0

    rows_dev = tokens.shape[0]
    group_len = rows_dev * lax.axis_size("tensor")
    place = jnp.where(jnp.arange(2) == 0, t, shard).astype(jnp.int32)
    prep = prepare(
        lengths,
        place,
        biases,
        frozen_norm_gains,
        adapter_down_weights,
        adapter_up_weights,
        rows_dev,
        group_len,
        dp_size,
    )
    small = [
        {
            "meta": prep["meta"],
            "ends": prep["ends"],
            "adapter": prep[f"adapter{l}"],
            "up": prep[f"up{l}"],
            "vecs": prep[f"vecs{l}"],
        }
        for l in range(ENCODER_LAYERS)
    ]

    packed = []

    def exchange_shards(l, with_share, gate=(), pack_gate=()):
        qkv = query_key_value_weight[l]
        own = [
            jnp.concatenate([qkv[0], qkv[1]], -1),
            jnp.concatenate([qkv[2], output_projection_weight[l]], -1),
        ]
        if with_share:
            share = lax.dynamic_slice(
                feedforward_out_weight, (l, shard * piece_rows, 0), (1, piece_rows, MODEL_WIDTH)
            )[0]
            own += [share[:, :SET_COLS], share[:, SET_COLS:]]
        own = jnp.stack(own)
        packed.append(own)
        other = after(swap(after(own, *gate), "tensor", 2), *pack_gate)
        first = jnp.where(upper == 0, own, other)
        second = jnp.where(upper == 0, other, own)
        parts = []
        for m in range(4):
            a = first[m // 2][:, (m % 2) * 192 : (m % 2 + 1) * 192]
            b = second[m // 2][:, (m % 2) * 192 : (m % 2 + 1) * 192]
            parts.append(jnp.concatenate([a[:, :128], b[:, :128], a[:, 128:], b[:, 128:]], -1))
        return jnp.concatenate([jnp.stack(parts), other[2:]])

    def gather_whole(piece):
        whole = lax.all_gather(piece, "dp", axis=1, tiled=True)
        return [whole], [swap(whole, "tensor", 1)]

    def gather_rows(rows, *earlier):
        other = swap(after(rows, *earlier), "tensor", 2)
        return [rows, swap(rows, "tensor", 1), other, swap(other, "tensor", 1)]

    def far_swap(weight, *earlier):
        return swap(after(weight, *earlier), "tensor", 2)

    bias_rows = jnp.pad(feedforward_bias, ((0, 14), (0, 0)))
    first_rows = jnp.concatenate([tokens, bias_rows])
    first_sib = swap(first_rows, "tensor", 1)
    piece0 = exchange_shards(0, True)
    in_sib = swap(after(feedforward_in_weight, packed[0]), "tensor", 1)
    out_sib = swap(after(feedforward_out_weight, packed[0]), "tensor", 1)
    piece0 = after(piece0, first_sib, in_sib, out_sib)
    if pieces_fit:
        ring0 = RingGather(piece0)
        ring0.step()
        ring0.other_core()
        ring0.step((prep["ends"],))
        while ring0.left():
            ring0.other_core()
            ring0.step()
        ring0.other_core()
        weights0 = ring0.got, ring0.sib
    else:
        weights0 = gather_whole(piece0)
    own0, sib0 = weights0
    first_far = swap(after(first_rows, piece0), "tensor", 2)
    x = [[first_rows, first_sib, first_far, swap(first_far, "tensor", 1)]]
    far_in0 = far_swap(feedforward_in_weight[0], first_far, *sib0[:3])

    def ff_weights(far_in, far_out, *gate):
        return (
            feedforward_in_weight,
            feedforward_out_weight,
            in_sib,
            out_sib,
            far_in,
            [swap(after(v, *gate), "tensor", 1) for v in far_in],
            far_out,
            [swap(after(v, *gate), "tensor", 1) for v in far_out],
            x[0],
        )

    state0 = attention_forward(x[0], weights0, small[0])
    f1 = state0["f1"]
    piece1 = exchange_shards(1, True, (first_far, *sib0[:3]), own0[4:6])
    ring1 = RingGather(piece1) if pieces_fit else None
    if ring1:
        first = ring1.step((own0[-1],))
        ring1.other_core(f1)
        ring1.step((f1,))
    else:
        weights1, first = gather_whole(piece1), ()
    half = MODEL_WIDTH // 2
    far_in1 = [far_swap(feedforward_in_weight[1, :half], far_in0)]
    ff_w = [ff_weights([far_in0], [], *first)]
    far_in1.append(far_swap(feedforward_in_weight[1, half:], far_in1[0]))
    ready = [far_in1[0], *(ring1.sib if ring1 else [])]
    state0.update(feedforward_forward(after(f1, *ready), weights0, ff_w[0], small[0], 0))
    z = state0["z"]
    x.append(gather_rows(z, far_in1[1]))
    if ring1:
        while ring1.left():
            ring1.step((z,))
        ring1.other_core(x[1][2])
        weights1 = ring1.got, ring1.sib
    ff_w.append(ff_weights(far_in1, [], x[1][2]))
    att_w = [weights0, weights1]
    saved = [state0, attention_forward(x[1], weights1, small[1])]

    last = ENCODER_LAYERS - 1
    gs = [final_output_gradient]
    sums = [None] * ENCODER_LAYERS
    for l in reversed(range(ENCODER_LAYERS)):
        out = layer_backward(gs, x[l], att_w[l], ff_w[l], saved[l], small[l], l, l == last)
        if l == last:
            activations = out["z"]
        p3 = swap(out["p3"], "tensor", 1)
        p1 = swap(out["p1"], "tensor", 1)
        p2 = swap((out["p2"].astype(F32) + p3.astype(F32)).astype(BF16), "tensor", 2)
        gs = [out["p0"], p1, p2]
        sums[l] = sum_all(out["grads"])

    input_grad = sum(g.astype(F32) for g in gs).astype(BF16)
    grad_a, grad_b = finish(sums)
    return activations, input_grad, grad_a, grad_b


def solution(mesh):
    return jax.shard_map(
        body,
        mesh=mesh,
        in_specs=(
            P(("dp", "tensor"), None),
            P(("dp", "tensor"), None),
            P("dp", None),
            P(None, None, "dp", "tensor"),
            P(None, "dp", "tensor"),
            P(),
            P(),
            P(None, None, "tensor"),
            P(None, "tensor"),
            P(None, "tensor", None),
            P(),
            P(),
        ),
        out_specs=(P(("dp", "tensor"), None), P(("dp", "tensor"), None), P(), P()),
        check_vma=False,
    )
```

```python
from types import SimpleNamespace

import jax
import jax.numpy as jnp
from jax import lax
from jax.experimental import pallas as pl
from jax.experimental.pallas import tpu as pltpu
from jax.sharding import PartitionSpec as P

MODEL_WIDTH = 768
HEAD_DIM = 64
ADAPTER_RANK = 8
ENCODER_LAYERS = 2
HEADS = 12
SET_COLS = 384
HEAD_GROUP = 12
KEY_BLOCK = 128
EPSILON = 1e-05
MASKED = -1000000000.0
VMEM_LIMIT = 56 * 1024 * 1024

F32 = jnp.float32
BF16 = jnp.bfloat16
ANY = pl.ANY
VMEM = pltpu.VMEM
SMEM = pltpu.SMEM


def dot_nn(a, b):
    return lax.dot_general(a, b, (((1,), (0,)), ((), ())), preferred_element_type=F32)


def dot_nt(a, b):
    return lax.dot_general(a, b, (((1,), (1,)), ((), ())), preferred_element_type=F32)


def dot_tn(a, b):
    return lax.dot_general(a, b, (((0,), (0,)), ((), ())), preferred_element_type=F32)


def aligned(start, size):
    return pl.ds(pl.multiple_of(start, size), size)


def run_kernel(name, kernel, inputs, outputs, scratch, flops, nbytes, spaces={}):
    flat, specs, layout = [], [], []
    for key, (space, value) in inputs.items():
        many = isinstance(value, list)
        values = value if many else [value]
        layout.append((key, len(values), many))
        flat += values
        specs += [pl.BlockSpec(memory_space=space)] * len(values)

    def whole(*refs):
        named, at = {}, 0
        for key, count, many in layout:
            named[key] = list(refs[at : at + count]) if many else refs[at]
            at += count
        for key in (*outputs, *scratch):
            named[key] = refs[at]
            at += 1
        kernel(SimpleNamespace(**named))

    result = pl.pallas_call(
        whole,
        out_shape=tuple(outputs.values()),
        in_specs=specs,
        out_specs=tuple(pl.BlockSpec(memory_space=spaces.get(k, VMEM)) for k in outputs),
        scratch_shapes=list(scratch.values()),
        compiler_params=pltpu.CompilerParams(vmem_limit_bytes=VMEM_LIMIT),
        cost_estimate=pl.CostEstimate(flops=flops, bytes_accessed=nbytes, transcendentals=0),
        name=name,
    )(*flat)
    return dict(zip(outputs, result))


class Queue:
    def __init__(self, ahead):
        self.ahead, self.groups, self.started = ahead, [], 0

    def add(self, copies):
        self.groups.append(copies)
        return len(self.groups) - 1

    def start_to(self, last):
        while self.started < min(last, len(self.groups)):
            for c in self.groups[self.started]:
                c.start()
            self.started += 1

    def wait(self, at):
        self.start_to(at + 1 + self.ahead)
        for c in self.groups[at]:
            c.wait()
        self.groups[at] = []


def piece_copies(pieces, source_of, target_of, sem, meta):
    out = []
    rows = MODEL_WIDTH // len(pieces)
    for k, piece in enumerate(pieces):
        if len(pieces) == 1:
            target = target_of(pl.ds(0, rows))
        else:
            target = target_of(aligned(meta[4 + k] * rows, rows))
        out.append(pltpu.make_async_copy(source_of(piece), target, sem))
    return out


def meta_of(r):
    return r.meta[0], r.meta[2], r.meta[3]


def attention_weight_copies(r):
    core = jnp.bitwise_and(r.meta[0], 1)
    out = []
    for m in range(4):
        copies = []
        for pieces, s in ((r.att_own, core), (r.att_sib, 1 - core)):
            copies += piece_copies(
                pieces,
                lambda p, m=m: p.at[m],
                lambda rows, m=m, s=s: r.w.at[m, s, rows],
                r.w_sem.at[m],
                r.meta,
            )
        out.append(copies)
    return out


def feedforward_weight_copies(r, layer):
    whole = (r.in_own.at[layer], r.out_own.at[layer], r.in_sib.at[layer], r.out_sib.at[layer])
    out = [[pltpu.make_async_copy(v, r.ff.at[m], r.ff_sem.at[m])] for m, v in enumerate(whole)]
    for m, value, far, pieces in (
        (4, r.in_far, r.out_far, r.att_own),
        (6, r.in_far_sib, r.out_far_sib, r.att_sib),
    ):
        copies, at = [], 0
        for part in value:
            rows = pl.ds(at, part.shape[0])
            copies.append(pltpu.make_async_copy(part, r.ff.at[m, rows], r.ff_sem.at[m]))
            at += part.shape[0]
        out.append(copies)
        if far:
            out.append([pltpu.make_async_copy(far[0], r.ff.at[m + 1], r.ff_sem.at[m + 1])])
            continue
        copies = []
        for half in range(2):
            cols = pl.ds(half * SET_COLS, SET_COLS)
            copies += piece_copies(
                pieces,
                lambda p, half=half: p.at[4 + half],
                lambda rows, m=m, cols=cols: r.ff.at[m + 1, rows, cols],
                r.ff_sem.at[m + 1],
                r.meta,
            )
        out.append(copies)
    return out


def bias_copies(r):
    rows = r.ends.shape[1]
    return [
        pltpu.make_async_copy(first.at[pl.ds(rows, 16)], r.bias_rows.at[j], r.bias_sem)
        for j, first in enumerate(r.first_rows)
    ]


def row_copies(r):
    t = r.meta[0]
    rows = r.ends.shape[1]
    return [
        pltpu.make_async_copy(
            r.rows[j].at[pl.ds(0, rows)], r.xs.at[aligned(jnp.bitwise_xor(t, j) * rows, rows)], r.x_sem.at[j]
        )
        for j in range(4)
    ]


def pair_cols(h):
    return slice((h // 2) * 128, (h // 2 + 1) * 128)


def head_cols(h):
    return slice(h * HEAD_DIM, (h + 1) * HEAD_DIM)


def keep_head(value, h):
    lane = lax.broadcasted_iota(jnp.int32, value.shape, 1)
    keep = (lane < HEAD_DIM) if h % 2 == 0 else (lane >= HEAD_DIM)
    return jnp.where(keep, value, jnp.zeros_like(value))


def key_mask(r, kb, rows):
    kpos = kb * KEY_BLOCK + lax.broadcasted_iota(jnp.int32, (KEY_BLOCK, rows), 0)
    return jnp.where((kpos >= r.ends[0:1]) & (kpos < r.ends[1:2]), 0.0, MASKED)


def attention_forward_stage(r, queue, rows_at, weights_at):
    t, low, high = meta_of(r)
    rows_dev = r.ends.shape[1]
    per = rows_dev // KEY_BLOCK
    own = aligned(t * rows_dev, rows_dev)
    for at in (rows_at, weights_at[1], weights_at[2]):
        queue.wait(at)

    def project_block(b, _):
        rows = aligned(b * rows_dev, rows_dev)
        xb = r.xs[rows]
        db = dot_nn(xb, r.adapter[...]).astype(BF16)
        r.down[rows] = db
        for s in range(2):
            cols = slice(s * SET_COLS, (s + 1) * SET_COLS)
            kb = dot_nn(xb, r.w[1, s]).astype(BF16)
            r.k[rows, cols] = kb
            kb_t = kb.T
            vb = (dot_nn(xb, r.w[2, s]) + dot_nn(db, r.up[1, :, cols]) + r.vecs[7:8, cols]).astype(BF16)
            r.v[rows, cols] = vb
            vb_t = vb.T
            for i in range(per):
                keys = slice(i * KEY_BLOCK, (i + 1) * KEY_BLOCK)
                r.kt[b * per + i, cols, :] = kb_t[:, keys]
                r.vt[b * per + i, cols, :] = vb_t[:, keys]
        return 0

    lax.fori_loop(low // rows_dev, (high + rows_dev - 1) // rows_dev, project_block, 0)

    queue.wait(weights_at[0])
    for s in range(2):
        cols = slice(s * SET_COLS, (s + 1) * SET_COLS)
        qv = dot_nn(r.xs[own], r.w[0, s]) + dot_nn(r.down[own], r.up[0, :, cols]) + r.vecs[6:7, cols]
        r.q[:, cols] = (qv * HEAD_DIM**-0.5).astype(BF16)
    for h in range(HEADS):
        r.qm[h] = keep_head(r.q[:, pair_cols(h)], h)
    r.acc[...] = jnp.zeros_like(r.acc)
    r.tops[...] = jnp.full_like(r.tops, -3e38)
    r.sums[...] = jnp.zeros_like(r.sums)

    def key_step(kb, _):
        keys = aligned(kb * KEY_BLOCK, KEY_BLOCK)
        mask = key_mask(r, kb, rows_dev)
        for first in range(0, HEADS, HEAD_GROUP):
            heads = range(first, first + HEAD_GROUP)
            s = [dot_nt(r.k[keys, pair_cols(h)], r.qm[h]) + mask for h in heads]
            old = [r.tops[h : h + 1] for h in heads]
            top = [jnp.maximum(o, jnp.max(v, axis=0, keepdims=True)) for o, v in zip(old, s)]
            fade = [jnp.exp(o - n) for o, n in zip(old, top)]
            p = [jnp.exp(v - n) for v, n in zip(s, top)]
            low_p = [v.astype(BF16) for v in p]
            for i, h in enumerate(heads):
                r.tops[h : h + 1] = top[i]
                r.sums[h : h + 1] = r.sums[h : h + 1] * fade[i] + jnp.sum(p[i], axis=0, keepdims=True)
            for i, h in enumerate(heads):
                cols = head_cols(h)
                r.acc[cols] = r.acc[cols] * fade[i] + dot_nn(r.vt[kb, cols, :], low_p[i])
        return 0

    lax.fori_loop(low // KEY_BLOCK, (high + KEY_BLOCK - 1) // KEY_BLOCK, key_step, 0)
    for h in range(HEADS):
        r.acc[head_cols(h)] = r.acc[head_cols(h)] / r.sums[h : h + 1]
    r.lse[...] = r.tops[...] + jnp.log(r.sums[...])
    r.c[...] = r.acc[...].T.astype(BF16)
    queue.wait(weights_at[3])
    f1 = r.xs[own].astype(F32) + r.vecs[0:1]
    for s in range(2):
        f1 = f1 + dot_nt(r.c[:, s * SET_COLS : (s + 1) * SET_COLS], r.w[3, s])
    r.f1[...] = f1


def struct(shape, dtype):
    return jax.ShapeDtypeStruct(shape, dtype)


def attention_inputs(x, weights, small):
    own, sib = weights
    return {
        "meta": (SMEM, small["meta"]),
        "ends": (VMEM, small["ends"]),
        "adapter": (VMEM, small["adapter"]),
        "up": (VMEM, small["up"]),
        "vecs": (VMEM, small["vecs"]),
        "rows": (ANY, x),
        "att_own": (ANY, own),
        "att_sib": (ANY, sib),
    }


def attention_scratch(rows):
    return {
        "xs": VMEM((4 * rows, MODEL_WIDTH), BF16),
        "w": VMEM((4, 2, MODEL_WIDTH, SET_COLS), BF16),
        "qm": VMEM((HEADS, rows, 128), BF16),
        "acc": VMEM((MODEL_WIDTH, rows), F32),
        "x_sem": pltpu.SemaphoreType.DMA((4,)),
        "w_sem": pltpu.SemaphoreType.DMA((4,)),
    }


def softmax_scratch(rows):
    return {
        "vt": VMEM((4 * rows // KEY_BLOCK, MODEL_WIDTH, KEY_BLOCK), BF16),
        "tops": VMEM((16, rows), F32),
        "sums": VMEM((16, rows), F32),
    }


def attention_forward(x, weights, small):
    rows = small["ends"].shape[1]
    group = 4 * rows
    blocks = group // KEY_BLOCK

    def kernel(r):
        queue = Queue(2)
        rows_at = queue.add(row_copies(r))
        copies = attention_weight_copies(r)
        weights_at = {m: queue.add(copies[m]) for m in (1, 2, 0, 3)}
        attention_forward_stage(r, queue, rows_at, weights_at)

    return run_kernel(
        "attention_forward",
        kernel,
        attention_inputs(x, weights, small),
        {
            "q": struct((rows, MODEL_WIDTH), BF16),
            "k": struct((group, MODEL_WIDTH), BF16),
            "v": struct((group, MODEL_WIDTH), BF16),
            "kt": struct((blocks, MODEL_WIDTH, KEY_BLOCK), BF16),
            "down": struct((group, 128), BF16),
            "lse": struct((16, rows), F32),
            "c": struct((rows, MODEL_WIDTH), BF16),
            "f1": struct((rows, MODEL_WIDTH), F32),
        },
        {
            **attention_scratch(rows),
            **softmax_scratch(rows),
        },
        8_000_000_000,
        12_000_000,
    )


def attention_backward_stage(r, queue, rows_at, state_at, weights_at):
    t, low, high = meta_of(r)
    rows_dev = r.ends.shape[1]
    block_low = low // rows_dev
    block_high = (high + rows_dev - 1) // rows_dev

    def clear_block(b, _):
        rows = aligned(b * rows_dev, rows_dev)
        r.gk[rows] = jnp.zeros((rows_dev, MODEL_WIDTH), F32)
        r.gv[rows] = jnp.zeros((rows_dev, MODEL_WIDTH), F32)
        return 0

    lax.fori_loop(block_low, block_high, clear_block, 0)
    r.acc[...] = jnp.zeros_like(r.acc)
    queue.wait(weights_at[3])
    gf1_low = r.gf1[...].astype(BF16)
    for s in range(2):
        r.gc[:, s * SET_COLS : (s + 1) * SET_COLS] = dot_nn(gf1_low, r.w[3, s]).astype(BF16)
    queue.wait(state_at)
    pick = (
        lax.broadcasted_iota(jnp.int32, (16, MODEL_WIDTH), 1) // HEAD_DIM
        == lax.broadcasted_iota(jnp.int32, (16, MODEL_WIDTH), 0)
    ).astype(BF16)
    product = r.gc[...].astype(F32) * r.c[...].astype(F32)
    product_high = product.astype(BF16)
    product_low = (product - product_high.astype(F32)).astype(BF16)
    r.delta[...] = dot_nt(pick, product_high) + dot_nt(pick, product_low)
    for h in range(HEADS):
        r.qm[h] = keep_head(r.q[:, pair_cols(h)], h)
        r.gcm[h] = keep_head(r.gc[:, pair_cols(h)], h)

    def key_step(kb, _):
        keys = aligned(kb * KEY_BLOCK, KEY_BLOCK)
        mask = key_mask(r, kb, rows_dev)
        for first in range(0, HEADS, HEAD_GROUP):
            heads = range(first, first + HEAD_GROUP)
            s = [dot_nt(r.k[keys, pair_cols(h)], r.qm[h]) + mask for h in heads]
            gp = [dot_nt(r.v[keys, pair_cols(h)], r.gcm[h]) for h in heads]
            p = [jnp.exp(v - r.lse[h : h + 1]) for h, v in zip(heads, s)]
            gs = [
                (pv * (gv - r.delta[h : h + 1])).astype(BF16) for h, pv, gv in zip(heads, p, gp)
            ]
            low_p = [v.astype(BF16) for v in p]
            for i, h in enumerate(heads):
                r.acc[head_cols(h)] += dot_nn(r.kt[kb, head_cols(h), :], gs[i])
            for i in range(0, HEAD_GROUP, 2):
                h = first + i
                cols = pair_cols(h)
                r.gk[keys, cols] += dot_nn(gs[i], r.qm[h]) + dot_nn(gs[i + 1], r.qm[h + 1])
                r.gv[keys, cols] += dot_nn(low_p[i], r.gcm[h]) + dot_nn(low_p[i + 1], r.gcm[h + 1])
        return 0

    lax.fori_loop(low // KEY_BLOCK, (high + KEY_BLOCK - 1) // KEY_BLOCK, key_step, 0)
    r.gc[...] = (r.acc[...].T * HEAD_DIM**-0.5).astype(BF16)

    for at in (rows_at, weights_at[0], weights_at[1], weights_at[2]):
        queue.wait(at)
    r.ga[...] = jnp.zeros_like(r.ga)
    r.gb[...] = jnp.zeros_like(r.gb)

    def key_value_gradient(b):
        rows = aligned(b * rows_dev, rows_dev)
        gkb = r.gk[rows].astype(BF16)
        gvb = r.gv[rows].astype(BF16)
        g = None
        for s in range(2):
            cols = slice(s * SET_COLS, (s + 1) * SET_COLS)
            term = dot_nt(gkb[:, cols], r.w[1, s]) + dot_nt(gvb[:, cols], r.w[2, s])
            g = term if g is None else g + term
        r.gb[1] += dot_tn(r.down[rows], gvb)
        return g, dot_nt(gvb, r.up[1])

    def add_adapter(b, g, gd):
        gd = gd.astype(BF16)
        r.ga[...] += dot_tn(gd, r.xs[aligned(b * rows_dev, rows_dev)])
        return g + dot_nt(gd, r.adapter[...])

    for j, out in ((2, r.p2), (3, r.p3), (1, r.p1)):
        b = jnp.bitwise_xor(t, j)
        used = (b >= block_low) & (b < block_high)

        @pl.when(used)
        def _(b=b, out=out):
            g, gd = key_value_gradient(b)
            out[...] = add_adapter(b, g, gd).astype(BF16)

        @pl.when(jnp.logical_not(used))
        def _(out=out):
            out[...] = jnp.zeros_like(out)

    g, gd = key_value_gradient(t)
    gq = r.gc[...]
    for s in range(2):
        g = g + dot_nt(gq[:, s * SET_COLS : (s + 1) * SET_COLS], r.w[0, s])
    gd = gd + dot_nt(gq, r.up[0])
    r.gb[0] += dot_tn(r.down[aligned(t * rows_dev, rows_dev)], gq)
    r.p0[...] = add_adapter(t, g, gd) + r.gf1[...]
    r.grads[0:16] = r.ga[0:16]
    r.grads[16:24] = whole_columns(r.gb[0, 0:8] * 2.0)
    r.grads[24:32] = whole_columns(r.gb[1, 8:16] * 2.0)


def norm_parts(v):
    mean = jnp.mean(v, axis=-1, keepdims=True)
    centered = v - mean
    rstd = lax.rsqrt(jnp.mean(centered * centered, axis=-1, keepdims=True) + EPSILON)
    return centered * rstd, rstd


def norm_back(g, gain, n, rstd):
    q = g * gain
    return rstd * (
        q - jnp.mean(q, axis=-1, keepdims=True) - n * jnp.mean(q * n, axis=-1, keepdims=True)
    )


def normal_cdf(u):
    z = jnp.abs(u) * 0.7071067811865476
    s = 1.0 / (1.0 + 0.3275911 * z)
    poly = s * (
        0.254829592
        + s * (-0.284496736 + s * (1.421413741 + s * (-1.453152027 + s * 1.061405429)))
    )
    e = jnp.exp(-z * z)
    tail = 0.5 * poly * e
    return jnp.where(u >= 0.0, 1.0 - tail, tail), e * 0.3989422804014327


def feedforward_forward_stage(r, queue, bias_at, weights_at, layer):
    n, _ = norm_parts(r.f1[...])
    y = n * r.vecs[4:5] + r.vecs[1:2]
    r.f2[...] = y + r.vecs[2:3]
    y_low = y.astype(BF16)
    queue.wait(bias_at)
    for j in range(4):
        r.ff_bias[j : j + 1] = r.bias_rows[j].astype(F32)[layer : layer + 1]
    for j in range(4):
        queue.wait(weights_at[2 * j])
        for part in range(3):
            cols = slice(part * 256, (part + 1) * 256)
            u = dot_nn(y_low, r.ff[2 * j, :, cols]) + r.ff_bias[j : j + 1, cols]
            cdf, density = normal_cdf(u)
            r.hid[j, :, cols] = (u * cdf).astype(BF16)
            r.slope[j, :, cols] = (cdf + u * density).astype(BF16)
    f2 = r.f2[...]
    for j in range(4):
        queue.wait(weights_at[2 * j + 1])
        f2 = f2 + dot_nn(r.hid[j], r.ff[2 * j + 1])
    r.f2[...] = f2
    n2, _ = norm_parts(f2)
    r.z[...] = (n2 * r.vecs[5:6] + r.vecs[3:4]).astype(BF16)


def feedforward_backward_stage(r, queue, weights_at):
    g = r.gs[0][...].astype(F32)
    for part in r.gs[1:]:
        g = g + part[...].astype(F32)
    n2, r2 = norm_parts(r.f2[...])
    gf2 = norm_back(g, r.vecs[5:6], n2, r2)
    r.gf1[...] = gf2
    gf2_low = gf2.astype(BF16)
    for j in range(4):
        queue.wait(weights_at[2 * j + 1])
        for part in range(3):
            cols = slice(part * 256, (part + 1) * 256)
            gh = dot_nt(gf2_low, r.ff[2 * j + 1, cols, :])
            r.hid[j, :, cols] = (gh * r.slope[j, :, cols].astype(F32)).astype(BF16)
    gy = r.gf1[...]
    for j in range(4):
        queue.wait(weights_at[2 * j])
        gy = gy + dot_nt(r.hid[j], r.ff[2 * j])
    n1, r1 = norm_parts(r.f1[...])
    r.gf1[...] = norm_back(gy, r.vecs[4:5], n1, r1)


def feedforward_scratch(rows):
    return {
        "ff": VMEM((8, MODEL_WIDTH, MODEL_WIDTH), BF16),
        "hid": VMEM((4, rows, MODEL_WIDTH), BF16),
        "ff_sem": pltpu.SemaphoreType.DMA((8,)),
        "bias_rows": VMEM((4, 16, MODEL_WIDTH), BF16),
        "ff_bias": VMEM((8, MODEL_WIDTH), F32),
        "bias_sem": pltpu.SemaphoreType.DMA,
    }


def feedforward_inputs(weights):
    names = ("in_own", "out_own", "in_sib", "out_sib", "in_far", "in_far_sib", "out_far", "out_far_sib", "first_rows")
    return {k: (ANY, v) for k, v in zip(names, weights)}


def feedforward_forward(f1, weights, ff_weights, small, layer):
    rows = f1.shape[0]

    def kernel(r):
        queue = Queue(3)
        bias_at = queue.add(bias_copies(r))
        copies = feedforward_weight_copies(r, layer)
        weights_at = {m: queue.add(copies[m]) for m in (0, 2, 4, 6, 1, 3, 5, 7)}
        queue.start_to(4)
        feedforward_forward_stage(r, queue, bias_at, weights_at, layer)

    return run_kernel(
        "feedforward_forward",
        kernel,
        {
            "meta": (SMEM, small["meta"]),
            "vecs": (VMEM, small["vecs"]),
            "ends": (VMEM, small["ends"]),
            "f1": (VMEM, f1),
            "att_own": (ANY, weights[0]),
            "att_sib": (ANY, weights[1]),
            **feedforward_inputs(ff_weights),
        },
        {
            "f2": struct((rows, MODEL_WIDTH), F32),
            "slope": struct((4, rows, MODEL_WIDTH), BF16),
            "z": struct((rows, MODEL_WIDTH), BF16),
        },
        feedforward_scratch(rows),
        6_000_000_000,
        12_000_000,
    )


def layer_backward(gs, x, weights, ff_weights, saved, small, layer, forward):
    rows = small["ends"].shape[1]
    group = 4 * rows
    blocks = group // KEY_BLOCK
    state = {
        "q": VMEM((rows, MODEL_WIDTH), BF16),
        "c": VMEM((rows, MODEL_WIDTH), BF16),
        "lse": VMEM((16, rows), F32),
        "k": VMEM((group, MODEL_WIDTH), BF16),
        "v": VMEM((group, MODEL_WIDTH), BF16),
        "kt": VMEM((blocks, MODEL_WIDTH, KEY_BLOCK), BF16),
        "down": VMEM((group, 128), BF16),
    }
    wide = {"f2": (rows, MODEL_WIDTH, F32), "slope": (4, rows, MODEL_WIDTH, BF16)}

    def kernel(r):
        queue = Queue(3)
        ff_copies = feedforward_weight_copies(r, layer)
        copies = attention_weight_copies(r)
        if forward:
            rows_at = queue.add(row_copies(r))
            weights_at = {m: queue.add(copies[m]) for m in (1, 2, 0, 3)}
            bias_at = queue.add(bias_copies(r))
            ff_at = {m: queue.add(ff_copies[m]) for m in (0, 2, 4, 6, 1, 3, 5, 7)}
            state_at = queue.add([])
            attention_forward_stage(r, queue, rows_at, weights_at)
            feedforward_forward_stage(r, queue, bias_at, ff_at, layer)
            feedforward_backward_stage(r, queue, ff_at)
            attention_backward_stage(r, queue, rows_at, state_at, weights_at)
            return
        ff_at = {m: queue.add(ff_copies[m]) for m in (1, 3, 5, 7, 0, 2, 4, 6)}
        queue.start_to(4)
        weights_at = {3: queue.add(copies[3])}
        state_at = queue.add(
            [
                pltpu.make_async_copy(getattr(r, "saved_" + k), getattr(r, k), r.state_sem)
                for k in state
            ]
        )
        rows_at = queue.add(row_copies(r))
        weights_at.update({m: queue.add(copies[m]) for m in (0, 1, 2)})
        feedforward_backward_stage(r, queue, ff_at)
        attention_backward_stage(r, queue, rows_at, state_at, weights_at)

    inputs = attention_inputs(x, weights, small)
    inputs["gs"] = (VMEM, gs)
    inputs.update(feedforward_inputs(ff_weights))
    block = struct((rows, MODEL_WIDTH), BF16)
    outputs = {
        "p0": struct((rows, MODEL_WIDTH), F32),
        "p1": block,
        "p2": block,
        "p3": block,
        "grads": struct((32, MODEL_WIDTH), F32),
    }
    scratch = {
        **attention_scratch(rows),
        **feedforward_scratch(rows),
        **state,
        "gf1": VMEM((rows, MODEL_WIDTH), F32),
        "gc": VMEM((rows, MODEL_WIDTH), BF16),
        "gcm": VMEM((HEADS, rows, 128), BF16),
        "delta": VMEM((16, rows), F32),
        "gk": VMEM((group, MODEL_WIDTH), F32),
        "gv": VMEM((group, MODEL_WIDTH), F32),
        "ga": VMEM((128, MODEL_WIDTH), F32),
        "gb": VMEM((2, 128, MODEL_WIDTH), F32),
        "state_sem": pltpu.SemaphoreType.DMA,
    }
    if forward:
        outputs["z"] = block
        scratch["f1"] = VMEM((rows, MODEL_WIDTH), F32)
        scratch["f2"] = VMEM((rows, MODEL_WIDTH), F32)
        scratch["slope"] = VMEM((4, rows, MODEL_WIDTH), BF16)
        scratch.update(softmax_scratch(rows))
    else:
        inputs["f1"] = (VMEM, saved["f1"])
        inputs.update({"saved_" + k: (ANY, saved[k]) for k in state})
        inputs["f2"] = (VMEM, saved["f2"])
        inputs["slope"] = (VMEM, saved["slope"])
    return run_kernel(
        "layer_backward", kernel, inputs, outputs, scratch, 20_000_000_000, 25_000_000
    )


def set_columns(value):
    def part(device, first, last):
        return value[..., device * 192 + first : device * 192 + last]

    out = []
    for s in range(2):
        out += [part(s, 0, 128), part(s + 2, 0, 128), part(s, 128, 192), part(s + 2, 128, 192)]
    return jnp.concatenate(out, -1)


def whole_columns(value):
    devices = [None] * 4
    for s in range(2):
        v = value[..., s * SET_COLS : (s + 1) * SET_COLS]
        devices[s] = jnp.concatenate([v[..., 0:128], v[..., 256:320]], -1)
        devices[s + 2] = jnp.concatenate([v[..., 128:256], v[..., 320:384]], -1)
    return jnp.concatenate(devices, -1)


def prepare(lengths, place, biases, gains, down, up, rows, group, size):
    slots = lengths.shape[1]
    order = ring_order(size)

    def kernel(r):
        t, shard = r.place[0], r.place[1]
        row = t * rows + lax.broadcasted_iota(jnp.int32, (1, rows), 1)
        start = jnp.zeros((1, rows), jnp.int32)
        stop = jnp.full((1, rows), group, jnp.int32)
        low, high, end = jnp.int32(0), jnp.int32(group), jnp.int32(0)
        for s in range(slots):
            end = end + r.lengths[0, s]
            start = jnp.where(end <= row, end, start)
            stop = jnp.where(end > row, jnp.minimum(stop, end), stop)
            low = jnp.where(end <= t * rows, end, low)
            high = jnp.where(end > t * rows + rows - 1, jnp.minimum(high, end), high)
        r.ends[0:1] = start
        r.ends[1:2] = stop
        r.meta[0] = t
        r.meta[1] = shard
        r.meta[2] = low
        r.meta[3] = high

        def device(position):
            out = jnp.int32(0)
            for k, d in enumerate(order):
                out = jnp.where(position == k, d, out)
            return out

        at = jnp.int32(0)
        for k, d in enumerate(order):
            at = jnp.where(shard == d, k, at)
        count = 4
        for step in range(size // 2 + 1):
            r.meta[count] = device(jnp.where(at - step < 0, at - step + size, at - step))
            count += 1
            if 0 < 2 * step < size:
                r.meta[count] = device(jnp.where(at + step >= size, at + step - size, at + step))
                count += 1

        lane = lax.broadcasted_iota(jnp.int32, (ADAPTER_RANK, 128), 1)
        sub = lax.broadcasted_iota(jnp.int32, (ADAPTER_RANK, 128), 0)
        none = jnp.zeros((ADAPTER_RANK, MODEL_WIDTH), F32)
        for l in range(ENCODER_LAYERS):
            both = jnp.zeros((MODEL_WIDTH, 128), F32)
            for m in range(2):
                put = (lane == sub + m * ADAPTER_RANK).astype(BF16)
                both = both + dot_tn(r.down[l, m], put)
            getattr(r, f"adapter{l}")[...] = both.astype(BF16)
            ups = getattr(r, f"up{l}")
            ups[...] = jnp.zeros_like(ups)
            for m in range(2):
                value = set_columns(r.up[l, m].astype(F32)) * 2.0
                value = jnp.concatenate([value, none] if m == 0 else [none, value], 0)
                ups[m, 0:16] = value.astype(BF16)
            vecs = getattr(r, f"vecs{l}")
            vecs[0:4] = r.biases[l, 2:6]
            vecs[4:6] = r.gains[l]
            vecs[6:8] = set_columns(r.biases[l, 0:2])

    outputs = {
        "meta": struct((4 + size,), jnp.int32),
        "ends": struct((2, rows), jnp.int32),
    }
    for l in range(ENCODER_LAYERS):
        outputs[f"adapter{l}"] = struct((MODEL_WIDTH, 128), BF16)
        outputs[f"up{l}"] = struct((2, 128, MODEL_WIDTH), BF16)
        outputs[f"vecs{l}"] = struct((8, MODEL_WIDTH), F32)
    return run_kernel(
        "prepare",
        kernel,
        {
            "lengths": (SMEM, lengths),
            "place": (SMEM, place),
            "biases": (VMEM, biases),
            "gains": (VMEM, gains),
            "down": (VMEM, down.swapaxes(2, 3)),
            "up": (VMEM, up),
        },
        outputs,
        {},
        100_000_000,
        2_000_000,
        {"meta": SMEM},
    )


def swap(value, axis, flip):
    size = lax.axis_size(axis)
    return lax.ppermute(value, axis, [(i, i ^ flip) for i in range(size)])


def ring_order(size):
    return list(range(0, size, 2)) + list(range(1, size, 2))[::-1]


class RingGather:
    def __init__(self, piece):
        self.size = lax.axis_size("dp")
        order = ring_order(self.size)
        self.up = [(order[i], order[(i + 1) % self.size]) for i in range(self.size)]
        self.down = [(b, a) for a, b in self.up]
        self.got, self.sib = [piece], []
        self.going_up = self.going_down = piece
        self.steps = 0

    def left(self):
        return self.steps < self.size // 2

    def step(self, gate=()):
        self.steps += 1
        self.going_up = lax.ppermute(after(self.going_up, *gate), "dp", self.up)
        out = [self.going_up]
        if 2 * self.steps < self.size:
            self.going_down = lax.ppermute(after(self.going_down, *gate), "dp", self.down)
            out.append(self.going_down)
        self.got += out
        return out

    def other_core(self, *gate):
        for value in self.got[len(self.sib) :]:
            self.sib.append(swap(after(value, *gate), "tensor", 1))


def after(value, *others):
    return lax.optimization_barrier((value, *others))[0] if others else value


def sum_all(first, second, late):
    lead = (lax.axis_index("tensor") & 1) == 0
    mine = jnp.where(lead, first, second).astype(BF16)
    value = mine.astype(F32) + swap(jnp.where(lead, second, first).astype(BF16), "tensor", 1).astype(F32)
    steps = []
    for axis, flip in (("dp", 1), ("tensor", 2)):
        while flip < lax.axis_size(axis):
            steps.append((axis, flip))
            flip *= 2
    for k, (axis, flip) in enumerate(steps):
        low = value.astype(BF16)
        if k == len(steps) - 1:
            low = after(low, late)
        value = low.astype(F32) + swap(low, axis, flip).astype(F32)
    other = swap(value, "tensor", 1)
    return jnp.where(lead, value, other), jnp.where(lead, other, value)


def body(
    tokens,
    final_output_gradient,
    lengths,
    query_key_value_weight,
    output_projection_weight,
    biases,
    frozen_norm_gains,
    feedforward_in_weight,
    feedforward_bias,
    feedforward_out_weight,
    adapter_down_weights,
    adapter_up_weights,
):
    dp_size = lax.axis_size("dp")
    t = lax.axis_index("tensor")
    shard = lax.axis_index("dp")
    upper = t >> 1
    piece_rows = MODEL_WIDTH // dp_size
    pieces_fit = piece_rows % 16 == 0 and dp_size & (dp_size - 1) == 0

    rows_dev = tokens.shape[0]
    group_len = rows_dev * lax.axis_size("tensor")
    place = jnp.where(jnp.arange(2) == 0, t, shard).astype(jnp.int32)
    prep = prepare(
        lengths,
        place,
        biases,
        frozen_norm_gains,
        adapter_down_weights,
        adapter_up_weights,
        rows_dev,
        group_len,
        dp_size,
    )
    small = [
        {
            "meta": prep["meta"],
            "ends": prep["ends"],
            "adapter": prep[f"adapter{l}"],
            "up": prep[f"up{l}"],
            "vecs": prep[f"vecs{l}"],
        }
        for l in range(ENCODER_LAYERS)
    ]

    packed = []

    def exchange_shards(l, with_share, gate=(), pack_gate=()):
        qkv = query_key_value_weight[l]
        own = [
            jnp.concatenate([qkv[0], qkv[1]], -1),
            jnp.concatenate([qkv[2], output_projection_weight[l]], -1),
        ]
        if with_share:
            share = lax.dynamic_slice(
                feedforward_out_weight, (l, shard * piece_rows, 0), (1, piece_rows, MODEL_WIDTH)
            )[0]
            own += [share[:, :SET_COLS], share[:, SET_COLS:]]
        own = jnp.stack(own)
        packed.append(own)
        other = after(swap(after(own, *gate), "tensor", 2), *pack_gate)
        first = jnp.where(upper == 0, own, other)
        second = jnp.where(upper == 0, other, own)
        parts = []
        for m in range(4):
            a = first[m // 2][:, (m % 2) * 192 : (m % 2 + 1) * 192]
            b = second[m // 2][:, (m % 2) * 192 : (m % 2 + 1) * 192]
            parts.append(jnp.concatenate([a[:, :128], b[:, :128], a[:, 128:], b[:, 128:]], -1))
        return jnp.concatenate([jnp.stack(parts), other[2:]])

    def gather_whole(piece):
        whole = lax.all_gather(piece, "dp", axis=1, tiled=True)
        return [whole], [swap(whole, "tensor", 1)]

    def gather_rows(rows, *earlier):
        other = swap(after(rows, *earlier), "tensor", 2)
        return [rows, swap(rows, "tensor", 1), other, swap(other, "tensor", 1)]

    def far_swap(weight, *earlier):
        return swap(after(weight, *earlier), "tensor", 2)

    bias_rows = jnp.pad(feedforward_bias, ((0, 14), (0, 0)))
    first_rows = jnp.concatenate([tokens, bias_rows])
    first_sib = swap(first_rows, "tensor", 1)
    piece0 = exchange_shards(0, True)
    in_sib = swap(after(feedforward_in_weight, packed[0]), "tensor", 1)
    out_sib = swap(after(feedforward_out_weight, packed[0]), "tensor", 1)
    piece0 = after(piece0, first_sib, in_sib, out_sib)
    if pieces_fit:
        ring0 = RingGather(piece0)
        ring0.step()
        ring0.other_core()
        ring0.step((prep["ends"],))
        while ring0.left():
            ring0.other_core()
            ring0.step()
        ring0.other_core()
        weights0 = ring0.got, ring0.sib
    else:
        weights0 = gather_whole(piece0)
    own0, sib0 = weights0
    first_far = swap(after(first_rows, piece0), "tensor", 2)
    x = [[first_rows, first_sib, first_far, swap(first_far, "tensor", 1)]]
    far_in0 = far_swap(feedforward_in_weight[0], first_far, *sib0[:3])

    def ff_weights(far_in, far_out, *gate):
        return (
            feedforward_in_weight,
            feedforward_out_weight,
            in_sib,
            out_sib,
            far_in,
            [swap(after(v, *gate), "tensor", 1) for v in far_in],
            far_out,
            [swap(after(v, *gate), "tensor", 1) for v in far_out],
            x[0],
        )

    state0 = attention_forward(x[0], weights0, small[0])
    f1 = state0["f1"]
    piece1 = exchange_shards(1, True, (first_far, *sib0[:3]), own0[4:6])
    ring1 = RingGather(piece1) if pieces_fit else None
    if ring1:
        first = ring1.step((own0[-1],))
        ring1.other_core(f1)
        ring1.step((f1,))
    else:
        weights1, first = gather_whole(piece1), ()
    half = MODEL_WIDTH // 2
    far_in1 = [far_swap(feedforward_in_weight[1, :half], own0[-1])]
    ff_w = [ff_weights([far_in0], [], *first)]
    far_in1.append(far_swap(feedforward_in_weight[1, half:], far_in1[0]))
    ready = [far_in1[0], *(ring1.sib if ring1 else [])]
    state0.update(feedforward_forward(after(f1, *ready), weights0, ff_w[0], small[0], 0))
    z = state0["z"]
    x.append(gather_rows(z, far_in1[1]))
    if ring1:
        while ring1.left():
            ring1.step((z,))
        ring1.other_core(x[1][2])
        weights1 = ring1.got, ring1.sib
    ff_w.append(ff_weights(far_in1, [], x[1][2]))
    att_w = [weights0, weights1]
    saved = [state0, None]

    last = ENCODER_LAYERS - 1
    gs = [final_output_gradient]
    grads = [None] * ENCODER_LAYERS
    for l in reversed(range(ENCODER_LAYERS)):
        out = layer_backward(gs, x[l], att_w[l], ff_w[l], saved[l], small[l], l, l == last)
        if l == last:
            activations = out["z"]
        p3 = swap(out["p3"], "tensor", 1)
        p1 = swap(out["p1"], "tensor", 1)
        far = (out["p2"].astype(F32) + p3.astype(F32)).astype(BF16)
        p2 = swap(far, "tensor", 2)
        gs = [out["p0"], p1, p2]
        grads[l] = out["grads"]

    input_grad = sum(g.astype(F32) for g in gs).astype(BF16)
    both = jnp.stack(sum_all(after(grads[0], far), grads[1], p2))
    shape = (ENCODER_LAYERS, 2, ADAPTER_RANK, MODEL_WIDTH)
    grad_a = both[:, :16].reshape(shape).swapaxes(2, 3)
    grad_b = both[:, 16:].reshape(shape)
    return activations, input_grad, grad_a, grad_b


def solution(mesh):
    return jax.shard_map(
        body,
        mesh=mesh,
        in_specs=(
            P(("dp", "tensor"), None),
            P(("dp", "tensor"), None),
            P("dp", None),
            P(None, None, "dp", "tensor"),
            P(None, "dp", "tensor"),
            P(),
            P(),
            P(None, None, "tensor"),
            P(None, "tensor"),
            P(None, "tensor", None),
            P(),
            P(),
        ),
        out_specs=(P(("dp", "tensor"), None), P(("dp", "tensor"), None), P(), P()),
        check_vma=False,
    )
```

```python
from types import SimpleNamespace

import jax
import jax.numpy as jnp
from jax import lax
from jax.experimental import pallas as pl
from jax.experimental.pallas import tpu as pltpu
from jax.sharding import PartitionSpec as P

MODEL_WIDTH = 768
HEAD_DIM = 64
ADAPTER_RANK = 8
ENCODER_LAYERS = 2
HEADS = 12
SET_COLS = 384
HEAD_GROUP = 12
KEY_BLOCK = 128
EPSILON = 1e-05
MASKED = -1000000000.0
VMEM_LIMIT = 56 * 1024 * 1024

F32 = jnp.float32
BF16 = jnp.bfloat16
ANY = pl.ANY
VMEM = pltpu.VMEM
SMEM = pltpu.SMEM


def dot_nn(a, b):
    return lax.dot_general(a, b, (((1,), (0,)), ((), ())), preferred_element_type=F32)


def dot_nt(a, b):
    return lax.dot_general(a, b, (((1,), (1,)), ((), ())), preferred_element_type=F32)


def dot_tn(a, b):
    return lax.dot_general(a, b, (((0,), (0,)), ((), ())), preferred_element_type=F32)


def aligned(start, size):
    return pl.ds(pl.multiple_of(start, size), size)


def run_kernel(name, kernel, inputs, outputs, scratch, flops, nbytes, spaces={}):
    flat, specs, layout = [], [], []
    for key, (space, value) in inputs.items():
        many = isinstance(value, list)
        values = value if many else [value]
        layout.append((key, len(values), many))
        flat += values
        specs += [pl.BlockSpec(memory_space=space)] * len(values)

    def whole(*refs):
        named, at = {}, 0
        for key, count, many in layout:
            named[key] = list(refs[at : at + count]) if many else refs[at]
            at += count
        for key in (*outputs, *scratch):
            named[key] = refs[at]
            at += 1
        kernel(SimpleNamespace(**named))

    result = pl.pallas_call(
        whole,
        out_shape=tuple(outputs.values()),
        in_specs=specs,
        out_specs=tuple(pl.BlockSpec(memory_space=spaces.get(k, VMEM)) for k in outputs),
        scratch_shapes=list(scratch.values()),
        compiler_params=pltpu.CompilerParams(vmem_limit_bytes=VMEM_LIMIT),
        cost_estimate=pl.CostEstimate(flops=flops, bytes_accessed=nbytes, transcendentals=0),
        name=name,
    )(*flat)
    return dict(zip(outputs, result))


class Queue:
    def __init__(self, ahead):
        self.ahead, self.groups, self.started = ahead, [], 0

    def add(self, copies):
        self.groups.append(copies)
        return len(self.groups) - 1

    def start_to(self, last):
        while self.started < min(last, len(self.groups)):
            for c in self.groups[self.started]:
                c.start()
            self.started += 1

    def wait(self, at):
        self.start_to(at + 1 + self.ahead)
        for c in self.groups[at]:
            c.wait()
        self.groups[at] = []


def piece_copies(pieces, source_of, target_of, sem, meta):
    out = []
    rows = MODEL_WIDTH // len(pieces)
    for k, piece in enumerate(pieces):
        if len(pieces) == 1:
            target = target_of(pl.ds(0, rows))
        else:
            target = target_of(aligned(meta[4 + k] * rows, rows))
        out.append(pltpu.make_async_copy(source_of(piece), target, sem))
    return out


def meta_of(r):
    return r.meta[0], r.meta[2], r.meta[3]


def attention_weight_copies(r):
    core = jnp.bitwise_and(r.meta[0], 1)
    out = []
    for m in range(4):
        copies = []
        for pieces, s in ((r.att_own, core), (r.att_sib, 1 - core)):
            copies += piece_copies(
                pieces,
                lambda p, m=m: p.at[m],
                lambda rows, m=m, s=s: r.w.at[m, s, rows],
                r.w_sem.at[m],
                r.meta,
            )
        out.append(copies)
    return out


def feedforward_weight_copies(r, layer):
    whole = (r.in_own.at[layer], r.out_own.at[layer], r.in_sib.at[layer], r.out_sib.at[layer])
    out = [[pltpu.make_async_copy(v, r.ff.at[m], r.ff_sem.at[m])] for m, v in enumerate(whole)]
    for m, value, far, pieces in (
        (4, r.in_far, r.out_far, r.att_own),
        (6, r.in_far_sib, r.out_far_sib, r.att_sib),
    ):
        copies, at = [], 0
        for part in value:
            rows = pl.ds(at, part.shape[0])
            copies.append(pltpu.make_async_copy(part, r.ff.at[m, rows], r.ff_sem.at[m]))
            at += part.shape[0]
        out.append(copies)
        if far:
            out.append([pltpu.make_async_copy(far[0], r.ff.at[m + 1], r.ff_sem.at[m + 1])])
            continue
        copies = []
        for half in range(2):
            cols = pl.ds(half * SET_COLS, SET_COLS)
            copies += piece_copies(
                pieces,
                lambda p, half=half: p.at[4 + half],
                lambda rows, m=m, cols=cols: r.ff.at[m + 1, rows, cols],
                r.ff_sem.at[m + 1],
                r.meta,
            )
        out.append(copies)
    return out


def bias_copies(r):
    rows = r.ends.shape[1]
    return [
        pltpu.make_async_copy(first.at[pl.ds(rows, 16)], r.bias_rows.at[j], r.bias_sem)
        for j, first in enumerate(r.first_rows)
    ]


def row_copies(r):
    t = r.meta[0]
    rows = r.ends.shape[1]
    return [
        pltpu.make_async_copy(
            r.rows[j].at[pl.ds(0, rows)], r.xs.at[aligned(jnp.bitwise_xor(t, j) * rows, rows)], r.x_sem.at[j]
        )
        for j in range(4)
    ]


def pair_cols(h):
    return slice((h // 2) * 128, (h // 2 + 1) * 128)


def head_cols(h):
    return slice(h * HEAD_DIM, (h + 1) * HEAD_DIM)


def keep_head(value, h):
    lane = lax.broadcasted_iota(jnp.int32, value.shape, 1)
    keep = (lane < HEAD_DIM) if h % 2 == 0 else (lane >= HEAD_DIM)
    return jnp.where(keep, value, jnp.zeros_like(value))


def key_mask(r, kb, rows):
    kpos = kb * KEY_BLOCK + lax.broadcasted_iota(jnp.int32, (KEY_BLOCK, rows), 0)
    return jnp.where((kpos >= r.ends[0:1]) & (kpos < r.ends[1:2]), 0.0, MASKED)


def attention_forward_stage(r, queue, rows_at, weights_at):
    t, low, high = meta_of(r)
    rows_dev = r.ends.shape[1]
    per = rows_dev // KEY_BLOCK
    own = aligned(t * rows_dev, rows_dev)
    for at in (rows_at, weights_at[1], weights_at[2]):
        queue.wait(at)

    def project_block(b, _):
        rows = aligned(b * rows_dev, rows_dev)
        xb = r.xs[rows]
        db = dot_nn(xb, r.adapter[...]).astype(BF16)
        r.down[rows] = db
        for s in range(2):
            cols = slice(s * SET_COLS, (s + 1) * SET_COLS)
            kb = dot_nn(xb, r.w[1, s]).astype(BF16)
            r.k[rows, cols] = kb
            kb_t = kb.T
            vb = (dot_nn(xb, r.w[2, s]) + dot_nn(db, r.up[1, :, cols]) + r.vecs[7:8, cols]).astype(BF16)
            r.v[rows, cols] = vb
            vb_t = vb.T
            for i in range(per):
                keys = slice(i * KEY_BLOCK, (i + 1) * KEY_BLOCK)
                r.kt[b * per + i, cols, :] = kb_t[:, keys]
                r.vt[b * per + i, cols, :] = vb_t[:, keys]
        return 0

    lax.fori_loop(low // rows_dev, (high + rows_dev - 1) // rows_dev, project_block, 0)

    queue.wait(weights_at[0])
    for s in range(2):
        cols = slice(s * SET_COLS, (s + 1) * SET_COLS)
        qv = dot_nn(r.xs[own], r.w[0, s]) + dot_nn(r.down[own], r.up[0, :, cols]) + r.vecs[6:7, cols]
        r.q[:, cols] = (qv * HEAD_DIM**-0.5).astype(BF16)
    for h in range(HEADS):
        r.qm[h] = keep_head(r.q[:, pair_cols(h)], h)
    r.acc[...] = jnp.zeros_like(r.acc)
    r.tops[...] = jnp.full_like(r.tops, -3e38)
    r.sums[...] = jnp.zeros_like(r.sums)

    def key_step(kb, _):
        keys = aligned(kb * KEY_BLOCK, KEY_BLOCK)
        mask = key_mask(r, kb, rows_dev)
        for first in range(0, HEADS, HEAD_GROUP):
            heads = range(first, first + HEAD_GROUP)
            s = [dot_nt(r.k[keys, pair_cols(h)], r.qm[h]) + mask for h in heads]
            old = [r.tops[h : h + 1] for h in heads]
            top = [jnp.maximum(o, jnp.max(v, axis=0, keepdims=True)) for o, v in zip(old, s)]
            fade = [jnp.exp(o - n) for o, n in zip(old, top)]
            p = [jnp.exp(v - n) for v, n in zip(s, top)]
            low_p = [v.astype(BF16) for v in p]
            for i, h in enumerate(heads):
                r.tops[h : h + 1] = top[i]
                r.sums[h : h + 1] = r.sums[h : h + 1] * fade[i] + jnp.sum(p[i], axis=0, keepdims=True)
            for i, h in enumerate(heads):
                cols = head_cols(h)
                r.acc[cols] = r.acc[cols] * fade[i] + dot_nn(r.vt[kb, cols, :], low_p[i])
        return 0

    lax.fori_loop(low // KEY_BLOCK, (high + KEY_BLOCK - 1) // KEY_BLOCK, key_step, 0)
    for h in range(HEADS):
        r.acc[head_cols(h)] = r.acc[head_cols(h)] / r.sums[h : h + 1]
    r.lse[...] = r.tops[...] + jnp.log(r.sums[...])
    r.c[...] = r.acc[...].T.astype(BF16)
    queue.wait(weights_at[3])
    f1 = r.xs[own].astype(F32) + r.vecs[0:1]
    for s in range(2):
        f1 = f1 + dot_nt(r.c[:, s * SET_COLS : (s + 1) * SET_COLS], r.w[3, s])
    r.f1[...] = f1


def struct(shape, dtype):
    return jax.ShapeDtypeStruct(shape, dtype)


def attention_inputs(x, weights, small):
    own, sib = weights
    return {
        "meta": (SMEM, small["meta"]),
        "ends": (VMEM, small["ends"]),
        "adapter": (VMEM, small["adapter"]),
        "up": (VMEM, small["up"]),
        "vecs": (VMEM, small["vecs"]),
        "rows": (ANY, x),
        "att_own": (ANY, own),
        "att_sib": (ANY, sib),
    }


def attention_scratch(rows):
    return {
        "xs": VMEM((4 * rows, MODEL_WIDTH), BF16),
        "w": VMEM((4, 2, MODEL_WIDTH, SET_COLS), BF16),
        "qm": VMEM((HEADS, rows, 128), BF16),
        "acc": VMEM((MODEL_WIDTH, rows), F32),
        "x_sem": pltpu.SemaphoreType.DMA((4,)),
        "w_sem": pltpu.SemaphoreType.DMA((4,)),
    }


def softmax_scratch(rows):
    return {
        "vt": VMEM((4 * rows // KEY_BLOCK, MODEL_WIDTH, KEY_BLOCK), BF16),
        "tops": VMEM((16, rows), F32),
        "sums": VMEM((16, rows), F32),
    }


def attention_forward(x, weights, small):
    rows = small["ends"].shape[1]
    group = 4 * rows
    blocks = group // KEY_BLOCK

    def kernel(r):
        queue = Queue(2)
        rows_at = queue.add(row_copies(r))
        copies = attention_weight_copies(r)
        weights_at = {m: queue.add(copies[m]) for m in (1, 2, 0, 3)}
        attention_forward_stage(r, queue, rows_at, weights_at)

    return run_kernel(
        "attention_forward",
        kernel,
        attention_inputs(x, weights, small),
        {
            "q": struct((rows, MODEL_WIDTH), BF16),
            "k": struct((group, MODEL_WIDTH), BF16),
            "v": struct((group, MODEL_WIDTH), BF16),
            "kt": struct((blocks, MODEL_WIDTH, KEY_BLOCK), BF16),
            "down": struct((group, 128), BF16),
            "lse": struct((16, rows), F32),
            "c": struct((rows, MODEL_WIDTH), BF16),
            "f1": struct((rows, MODEL_WIDTH), F32),
        },
        {
            **attention_scratch(rows),
            **softmax_scratch(rows),
        },
        8_000_000_000,
        12_000_000,
    )


def attention_backward_stage(r, queue, rows_at, state_at, weights_at):
    t, low, high = meta_of(r)
    rows_dev = r.ends.shape[1]
    block_low = low // rows_dev
    block_high = (high + rows_dev - 1) // rows_dev

    def clear_block(b, _):
        rows = aligned(b * rows_dev, rows_dev)
        r.gk[rows] = jnp.zeros((rows_dev, MODEL_WIDTH), F32)
        r.gv[rows] = jnp.zeros((rows_dev, MODEL_WIDTH), F32)
        return 0

    lax.fori_loop(block_low, block_high, clear_block, 0)
    r.acc[...] = jnp.zeros_like(r.acc)
    queue.wait(weights_at[3])
    gf1_low = r.gf1[...].astype(BF16)
    for s in range(2):
        r.gc[:, s * SET_COLS : (s + 1) * SET_COLS] = dot_nn(gf1_low, r.w[3, s]).astype(BF16)
    queue.wait(state_at)
    pick = (
        lax.broadcasted_iota(jnp.int32, (16, MODEL_WIDTH), 1) // HEAD_DIM
        == lax.broadcasted_iota(jnp.int32, (16, MODEL_WIDTH), 0)
    ).astype(BF16)
    product = r.gc[...].astype(F32) * r.c[...].astype(F32)
    product_high = product.astype(BF16)
    product_low = (product - product_high.astype(F32)).astype(BF16)
    r.delta[...] = dot_nt(pick, product_high) + dot_nt(pick, product_low)
    for h in range(HEADS):
        r.qm[h] = keep_head(r.q[:, pair_cols(h)], h)
        r.gcm[h] = keep_head(r.gc[:, pair_cols(h)], h)

    def key_step(kb, _):
        keys = aligned(kb * KEY_BLOCK, KEY_BLOCK)
        mask = key_mask(r, kb, rows_dev)
        for first in range(0, HEADS, HEAD_GROUP):
            heads = range(first, first + HEAD_GROUP)
            s = [dot_nt(r.k[keys, pair_cols(h)], r.qm[h]) + mask for h in heads]
            gp = [dot_nt(r.v[keys, pair_cols(h)], r.gcm[h]) for h in heads]
            p = [jnp.exp(v - r.lse[h : h + 1]) for h, v in zip(heads, s)]
            gs = [
                (pv * (gv - r.delta[h : h + 1])).astype(BF16) for h, pv, gv in zip(heads, p, gp)
            ]
            low_p = [v.astype(BF16) for v in p]
            for i, h in enumerate(heads):
                r.acc[head_cols(h)] += dot_nn(r.kt[kb, head_cols(h), :], gs[i])
            for i in range(0, HEAD_GROUP, 2):
                h = first + i
                cols = pair_cols(h)
                r.gk[keys, cols] += dot_nn(gs[i], r.qm[h]) + dot_nn(gs[i + 1], r.qm[h + 1])
                r.gv[keys, cols] += dot_nn(low_p[i], r.gcm[h]) + dot_nn(low_p[i + 1], r.gcm[h + 1])
        return 0

    lax.fori_loop(low // KEY_BLOCK, (high + KEY_BLOCK - 1) // KEY_BLOCK, key_step, 0)
    r.gc[...] = (r.acc[...].T * HEAD_DIM**-0.5).astype(BF16)

    for at in (rows_at, weights_at[0], weights_at[1], weights_at[2]):
        queue.wait(at)
    r.ga[...] = jnp.zeros_like(r.ga)
    r.gb[...] = jnp.zeros_like(r.gb)

    def key_value_gradient(b):
        rows = aligned(b * rows_dev, rows_dev)
        gkb = r.gk[rows].astype(BF16)
        gvb = r.gv[rows].astype(BF16)
        g = None
        for s in range(2):
            cols = slice(s * SET_COLS, (s + 1) * SET_COLS)
            term = dot_nt(gkb[:, cols], r.w[1, s]) + dot_nt(gvb[:, cols], r.w[2, s])
            g = term if g is None else g + term
        r.gb[1] += dot_tn(r.down[rows], gvb)
        return g, dot_nt(gvb, r.up[1])

    def add_adapter(b, g, gd):
        gd = gd.astype(BF16)
        r.ga[...] += dot_tn(gd, r.xs[aligned(b * rows_dev, rows_dev)])
        return g + dot_nt(gd, r.adapter[...])

    for j, out in ((2, r.p2), (3, r.p3), (1, r.p1)):
        b = jnp.bitwise_xor(t, j)
        used = (b >= block_low) & (b < block_high)

        @pl.when(used)
        def _(b=b, out=out):
            g, gd = key_value_gradient(b)
            out[...] = add_adapter(b, g, gd).astype(BF16)

        @pl.when(jnp.logical_not(used))
        def _(out=out):
            out[...] = jnp.zeros_like(out)

    g, gd = key_value_gradient(t)
    gq = r.gc[...]
    for s in range(2):
        g = g + dot_nt(gq[:, s * SET_COLS : (s + 1) * SET_COLS], r.w[0, s])
    gd = gd + dot_nt(gq, r.up[0])
    r.gb[0] += dot_tn(r.down[aligned(t * rows_dev, rows_dev)], gq)
    r.p0[...] = add_adapter(t, g, gd) + r.gf1[...]
    r.grads[0:16] = r.ga[0:16]
    r.grads[16:24] = whole_columns(r.gb[0, 0:8] * 2.0)
    r.grads[24:32] = whole_columns(r.gb[1, 8:16] * 2.0)


def norm_parts(v):
    mean = jnp.mean(v, axis=-1, keepdims=True)
    centered = v - mean
    rstd = lax.rsqrt(jnp.mean(centered * centered, axis=-1, keepdims=True) + EPSILON)
    return centered * rstd, rstd


def norm_back(g, gain, n, rstd):
    q = g * gain
    return rstd * (
        q - jnp.mean(q, axis=-1, keepdims=True) - n * jnp.mean(q * n, axis=-1, keepdims=True)
    )


def normal_cdf(u):
    z = jnp.abs(u) * 0.7071067811865476
    s = 1.0 / (1.0 + 0.3275911 * z)
    poly = s * (
        0.254829592
        + s * (-0.284496736 + s * (1.421413741 + s * (-1.453152027 + s * 1.061405429)))
    )
    e = jnp.exp(-z * z)
    tail = 0.5 * poly * e
    return jnp.where(u >= 0.0, 1.0 - tail, tail), e * 0.3989422804014327


def feedforward_forward_stage(r, queue, bias_at, weights_at, layer):
    n, _ = norm_parts(r.f1[...])
    y = n * r.vecs[4:5] + r.vecs[1:2]
    r.f2[...] = y + r.vecs[2:3]
    y_low = y.astype(BF16)
    queue.wait(bias_at)
    for j in range(4):
        r.ff_bias[j : j + 1] = r.bias_rows[j].astype(F32)[layer : layer + 1]
    for j in range(4):
        queue.wait(weights_at[2 * j])
        for part in range(3):
            cols = slice(part * 256, (part + 1) * 256)
            u = dot_nn(y_low, r.ff[2 * j, :, cols]) + r.ff_bias[j : j + 1, cols]
            cdf, density = normal_cdf(u)
            r.hid[j, :, cols] = (u * cdf).astype(BF16)
            r.slope[j, :, cols] = (cdf + u * density).astype(BF16)
    f2 = r.f2[...]
    for j in range(4):
        queue.wait(weights_at[2 * j + 1])
        f2 = f2 + dot_nn(r.hid[j], r.ff[2 * j + 1])
    r.f2[...] = f2
    n2, _ = norm_parts(f2)
    r.z[...] = (n2 * r.vecs[5:6] + r.vecs[3:4]).astype(BF16)


def feedforward_backward_stage(r, queue, weights_at):
    g = r.gs[0][...].astype(F32)
    for part in r.gs[1:]:
        g = g + part[...].astype(F32)
    n2, r2 = norm_parts(r.f2[...])
    gf2 = norm_back(g, r.vecs[5:6], n2, r2)
    r.gf1[...] = gf2
    gf2_low = gf2.astype(BF16)
    for j in range(4):
        queue.wait(weights_at[2 * j + 1])
        for part in range(3):
            cols = slice(part * 256, (part + 1) * 256)
            gh = dot_nt(gf2_low, r.ff[2 * j + 1, cols, :])
            r.hid[j, :, cols] = (gh * r.slope[j, :, cols].astype(F32)).astype(BF16)
    gy = r.gf1[...]
    for j in range(4):
        queue.wait(weights_at[2 * j])
        gy = gy + dot_nt(r.hid[j], r.ff[2 * j])
    n1, r1 = norm_parts(r.f1[...])
    r.gf1[...] = norm_back(gy, r.vecs[4:5], n1, r1)


def feedforward_scratch(rows):
    return {
        "ff": VMEM((8, MODEL_WIDTH, MODEL_WIDTH), BF16),
        "hid": VMEM((4, rows, MODEL_WIDTH), BF16),
        "ff_sem": pltpu.SemaphoreType.DMA((8,)),
        "bias_rows": VMEM((4, 16, MODEL_WIDTH), BF16),
        "ff_bias": VMEM((8, MODEL_WIDTH), F32),
        "bias_sem": pltpu.SemaphoreType.DMA,
    }


def feedforward_inputs(weights):
    names = ("in_own", "out_own", "in_sib", "out_sib", "in_far", "in_far_sib", "out_far", "out_far_sib", "first_rows")
    return {k: (ANY, v) for k, v in zip(names, weights)}


def feedforward_forward(f1, weights, ff_weights, small, layer):
    rows = f1.shape[0]

    def kernel(r):
        queue = Queue(3)
        bias_at = queue.add(bias_copies(r))
        copies = feedforward_weight_copies(r, layer)
        weights_at = {m: queue.add(copies[m]) for m in (0, 2, 4, 6, 1, 3, 5, 7)}
        queue.start_to(4)
        feedforward_forward_stage(r, queue, bias_at, weights_at, layer)

    return run_kernel(
        "feedforward_forward",
        kernel,
        {
            "meta": (SMEM, small["meta"]),
            "vecs": (VMEM, small["vecs"]),
            "ends": (VMEM, small["ends"]),
            "f1": (VMEM, f1),
            "att_own": (ANY, weights[0]),
            "att_sib": (ANY, weights[1]),
            **feedforward_inputs(ff_weights),
        },
        {
            "f2": struct((rows, MODEL_WIDTH), F32),
            "slope": struct((4, rows, MODEL_WIDTH), BF16),
            "z": struct((rows, MODEL_WIDTH), BF16),
        },
        feedforward_scratch(rows),
        6_000_000_000,
        12_000_000,
    )


def layer_backward(gs, x, weights, ff_weights, saved, small, layer, forward):
    rows = small["ends"].shape[1]
    group = 4 * rows
    blocks = group // KEY_BLOCK
    state = {
        "q": VMEM((rows, MODEL_WIDTH), BF16),
        "c": VMEM((rows, MODEL_WIDTH), BF16),
        "lse": VMEM((16, rows), F32),
        "k": VMEM((group, MODEL_WIDTH), BF16),
        "v": VMEM((group, MODEL_WIDTH), BF16),
        "kt": VMEM((blocks, MODEL_WIDTH, KEY_BLOCK), BF16),
        "down": VMEM((group, 128), BF16),
    }
    wide = {"f2": (rows, MODEL_WIDTH, F32), "slope": (4, rows, MODEL_WIDTH, BF16)}

    def kernel(r):
        queue = Queue(3)
        ff_copies = feedforward_weight_copies(r, layer)
        copies = attention_weight_copies(r)
        if forward:
            rows_at = queue.add(row_copies(r))
            weights_at = {m: queue.add(copies[m]) for m in (1, 2, 0, 3)}
            bias_at = queue.add(bias_copies(r))
            ff_at = {m: queue.add(ff_copies[m]) for m in (0, 2, 4, 6, 1, 3, 5, 7)}
            state_at = queue.add([])
            attention_forward_stage(r, queue, rows_at, weights_at)
            feedforward_forward_stage(r, queue, bias_at, ff_at, layer)
            feedforward_backward_stage(r, queue, ff_at)
            attention_backward_stage(r, queue, rows_at, state_at, weights_at)
            return
        for j in range(4):
            ff_copies[2 * j + 1].append(
                pltpu.make_async_copy(r.saved_slope.at[j], r.slope.at[j], r.slope_sem.at[j])
            )
        ff_at = {m: queue.add(ff_copies[m]) for m in (1, 3, 5, 7, 0, 2, 4, 6)}
        queue.start_to(4)
        weights_at = {3: queue.add(copies[3])}
        state_at = queue.add(
            [
                pltpu.make_async_copy(getattr(r, "saved_" + k), getattr(r, k), r.state_sem)
                for k in state
            ]
        )
        rows_at = queue.add(row_copies(r))
        weights_at.update({m: queue.add(copies[m]) for m in (0, 1, 2)})
        feedforward_backward_stage(r, queue, ff_at)
        attention_backward_stage(r, queue, rows_at, state_at, weights_at)

    inputs = attention_inputs(x, weights, small)
    inputs["gs"] = (VMEM, gs)
    inputs.update(feedforward_inputs(ff_weights))
    block = struct((rows, MODEL_WIDTH), BF16)
    outputs = {
        "p0": struct((rows, MODEL_WIDTH), F32),
        "p1": block,
        "p2": block,
        "p3": block,
        "grads": struct((32, MODEL_WIDTH), F32),
    }
    scratch = {
        **attention_scratch(rows),
        **feedforward_scratch(rows),
        **state,
        "gf1": VMEM((rows, MODEL_WIDTH), F32),
        "gc": VMEM((rows, MODEL_WIDTH), BF16),
        "gcm": VMEM((HEADS, rows, 128), BF16),
        "delta": VMEM((16, rows), F32),
        "gk": VMEM((group, MODEL_WIDTH), F32),
        "gv": VMEM((group, MODEL_WIDTH), F32),
        "ga": VMEM((128, MODEL_WIDTH), F32),
        "gb": VMEM((2, 128, MODEL_WIDTH), F32),
        "state_sem": pltpu.SemaphoreType.DMA,
    }
    if forward:
        outputs["z"] = block
        scratch["f1"] = VMEM((rows, MODEL_WIDTH), F32)
        scratch["f2"] = VMEM((rows, MODEL_WIDTH), F32)
        scratch["slope"] = VMEM((4, rows, MODEL_WIDTH), BF16)
        scratch.update(softmax_scratch(rows))
    else:
        inputs["f1"] = (VMEM, saved["f1"])
        inputs.update({"saved_" + k: (ANY, saved[k]) for k in state})
        inputs["f2"] = (VMEM, saved["f2"])
        inputs["saved_slope"] = (ANY, saved["slope"])
        scratch["slope"] = VMEM((4, rows, MODEL_WIDTH), BF16)
        scratch["slope_sem"] = pltpu.SemaphoreType.DMA((4,))
    return run_kernel(
        "layer_backward", kernel, inputs, outputs, scratch, 20_000_000_000, 25_000_000
    )


def set_columns(value):
    def part(device, first, last):
        return value[..., device * 192 + first : device * 192 + last]

    out = []
    for s in range(2):
        out += [part(s, 0, 128), part(s + 2, 0, 128), part(s, 128, 192), part(s + 2, 128, 192)]
    return jnp.concatenate(out, -1)


def whole_columns(value):
    devices = [None] * 4
    for s in range(2):
        v = value[..., s * SET_COLS : (s + 1) * SET_COLS]
        devices[s] = jnp.concatenate([v[..., 0:128], v[..., 256:320]], -1)
        devices[s + 2] = jnp.concatenate([v[..., 128:256], v[..., 320:384]], -1)
    return jnp.concatenate(devices, -1)


def prepare(lengths, place, biases, gains, down, up, rows, group, size):
    slots = lengths.shape[1]
    order = ring_order(size)

    def kernel(r):
        t, shard = r.place[0], r.place[1]
        row = t * rows + lax.broadcasted_iota(jnp.int32, (1, rows), 1)
        start = jnp.zeros((1, rows), jnp.int32)
        stop = jnp.full((1, rows), group, jnp.int32)
        low, high, end = jnp.int32(0), jnp.int32(group), jnp.int32(0)
        for s in range(slots):
            end = end + r.lengths[0, s]
            start = jnp.where(end <= row, end, start)
            stop = jnp.where(end > row, jnp.minimum(stop, end), stop)
            low = jnp.where(end <= t * rows, end, low)
            high = jnp.where(end > t * rows + rows - 1, jnp.minimum(high, end), high)
        r.ends[0:1] = start
        r.ends[1:2] = stop
        r.meta[0] = t
        r.meta[1] = shard
        r.meta[2] = low
        r.meta[3] = high

        def device(position):
            out = jnp.int32(0)
            for k, d in enumerate(order):
                out = jnp.where(position == k, d, out)
            return out

        at = jnp.int32(0)
        for k, d in enumerate(order):
            at = jnp.where(shard == d, k, at)
        count = 4
        for step in range(size // 2 + 1):
            r.meta[count] = device(jnp.where(at - step < 0, at - step + size, at - step))
            count += 1
            if 0 < 2 * step < size:
                r.meta[count] = device(jnp.where(at + step >= size, at + step - size, at + step))
                count += 1

        lane = lax.broadcasted_iota(jnp.int32, (ADAPTER_RANK, 128), 1)
        sub = lax.broadcasted_iota(jnp.int32, (ADAPTER_RANK, 128), 0)
        none = jnp.zeros((ADAPTER_RANK, MODEL_WIDTH), F32)
        for l in range(ENCODER_LAYERS):
            both = jnp.zeros((MODEL_WIDTH, 128), F32)
            for m in range(2):
                put = (lane == sub + m * ADAPTER_RANK).astype(BF16)
                both = both + dot_tn(r.down[l, m], put)
            getattr(r, f"adapter{l}")[...] = both.astype(BF16)
            ups = getattr(r, f"up{l}")
            ups[...] = jnp.zeros_like(ups)
            for m in range(2):
                value = set_columns(r.up[l, m].astype(F32)) * 2.0
                value = jnp.concatenate([value, none] if m == 0 else [none, value], 0)
                ups[m, 0:16] = value.astype(BF16)
            vecs = getattr(r, f"vecs{l}")
            vecs[0:4] = r.biases[l, 2:6]
            vecs[4:6] = r.gains[l]
            vecs[6:8] = set_columns(r.biases[l, 0:2])

    outputs = {
        "meta": struct((4 + size,), jnp.int32),
        "ends": struct((2, rows), jnp.int32),
    }
    for l in range(ENCODER_LAYERS):
        outputs[f"adapter{l}"] = struct((MODEL_WIDTH, 128), BF16)
        outputs[f"up{l}"] = struct((2, 128, MODEL_WIDTH), BF16)
        outputs[f"vecs{l}"] = struct((8, MODEL_WIDTH), F32)
    return run_kernel(
        "prepare",
        kernel,
        {
            "lengths": (SMEM, lengths),
            "place": (SMEM, place),
            "biases": (VMEM, biases),
            "gains": (VMEM, gains),
            "down": (VMEM, down.swapaxes(2, 3)),
            "up": (VMEM, up),
        },
        outputs,
        {},
        100_000_000,
        2_000_000,
        {"meta": SMEM},
    )


def swap(value, axis, flip):
    size = lax.axis_size(axis)
    return lax.ppermute(value, axis, [(i, i ^ flip) for i in range(size)])


def ring_order(size):
    return list(range(0, size, 2)) + list(range(1, size, 2))[::-1]


class RingGather:
    def __init__(self, piece):
        self.size = lax.axis_size("dp")
        order = ring_order(self.size)
        self.up = [(order[i], order[(i + 1) % self.size]) for i in range(self.size)]
        self.down = [(b, a) for a, b in self.up]
        self.got, self.sib = [piece], []
        self.going_up = self.going_down = piece
        self.steps = 0

    def left(self):
        return self.steps < self.size // 2

    def step(self, gate=()):
        self.steps += 1
        self.going_up = lax.ppermute(after(self.going_up, *gate), "dp", self.up)
        out = [self.going_up]
        if 2 * self.steps < self.size:
            self.going_down = lax.ppermute(after(self.going_down, *gate), "dp", self.down)
            out.append(self.going_down)
        self.got += out
        return out

    def other_core(self, *gate):
        for value in self.got[len(self.sib) :]:
            self.sib.append(swap(after(value, *gate), "tensor", 1))


def after(value, *others):
    return lax.optimization_barrier((value, *others))[0] if others else value


def sum_all(first, second, late):
    lead = (lax.axis_index("tensor") & 1) == 0
    mine = jnp.where(lead, first, second).astype(BF16)
    value = mine.astype(F32) + swap(jnp.where(lead, second, first).astype(BF16), "tensor", 1).astype(F32)
    steps = []
    for axis, flip in (("dp", 1), ("tensor", 2)):
        while flip < lax.axis_size(axis):
            steps.append((axis, flip))
            flip *= 2
    for k, (axis, flip) in enumerate(steps):
        low = value.astype(BF16)
        if k == len(steps) - 1:
            low = after(low, late)
        value = low.astype(F32) + swap(low, axis, flip).astype(F32)
    other = swap(value, "tensor", 1)
    return jnp.where(lead, value, other), jnp.where(lead, other, value)


def body(
    tokens,
    final_output_gradient,
    lengths,
    query_key_value_weight,
    output_projection_weight,
    biases,
    frozen_norm_gains,
    feedforward_in_weight,
    feedforward_bias,
    feedforward_out_weight,
    adapter_down_weights,
    adapter_up_weights,
):
    dp_size = lax.axis_size("dp")
    t = lax.axis_index("tensor")
    shard = lax.axis_index("dp")
    upper = t >> 1
    piece_rows = MODEL_WIDTH // dp_size
    pieces_fit = piece_rows % 16 == 0 and dp_size & (dp_size - 1) == 0

    rows_dev = tokens.shape[0]
    group_len = rows_dev * lax.axis_size("tensor")
    place = jnp.where(jnp.arange(2) == 0, t, shard).astype(jnp.int32)
    prep = prepare(
        lengths,
        place,
        biases,
        frozen_norm_gains,
        adapter_down_weights,
        adapter_up_weights,
        rows_dev,
        group_len,
        dp_size,
    )
    small = [
        {
            "meta": prep["meta"],
            "ends": prep["ends"],
            "adapter": prep[f"adapter{l}"],
            "up": prep[f"up{l}"],
            "vecs": prep[f"vecs{l}"],
        }
        for l in range(ENCODER_LAYERS)
    ]

    packed = []

    def exchange_shards(l, with_share, gate=(), pack_gate=()):
        qkv = query_key_value_weight[l]
        own = [
            jnp.concatenate([qkv[0], qkv[1]], -1),
            jnp.concatenate([qkv[2], output_projection_weight[l]], -1),
        ]
        if with_share:
            share = lax.dynamic_slice(
                feedforward_out_weight, (l, shard * piece_rows, 0), (1, piece_rows, MODEL_WIDTH)
            )[0]
            own += [share[:, :SET_COLS], share[:, SET_COLS:]]
        own = jnp.stack(own)
        packed.append(own)
        other = after(swap(after(own, *gate), "tensor", 2), *pack_gate)
        first = jnp.where(upper == 0, own, other)
        second = jnp.where(upper == 0, other, own)
        parts = []
        for m in range(4):
            a = first[m // 2][:, (m % 2) * 192 : (m % 2 + 1) * 192]
            b = second[m // 2][:, (m % 2) * 192 : (m % 2 + 1) * 192]
            parts.append(jnp.concatenate([a[:, :128], b[:, :128], a[:, 128:], b[:, 128:]], -1))
        return jnp.concatenate([jnp.stack(parts), other[2:]])

    def gather_whole(piece):
        whole = lax.all_gather(piece, "dp", axis=1, tiled=True)
        return [whole], [swap(whole, "tensor", 1)]

    def gather_rows(rows, *earlier):
        other = swap(after(rows, *earlier), "tensor", 2)
        return [rows, swap(rows, "tensor", 1), other, swap(other, "tensor", 1)]

    def far_swap(weight, *earlier):
        return swap(after(weight, *earlier), "tensor", 2)

    bias_rows = jnp.pad(feedforward_bias, ((0, 14), (0, 0)))
    first_rows = jnp.concatenate([tokens, bias_rows])
    first_sib = swap(first_rows, "tensor", 1)
    piece0 = exchange_shards(0, True)
    in_sib = swap(after(feedforward_in_weight, packed[0]), "tensor", 1)
    out_sib = swap(after(feedforward_out_weight, packed[0]), "tensor", 1)
    piece0 = after(piece0, first_sib, in_sib, out_sib)
    if pieces_fit:
        ring0 = RingGather(piece0)
        ring0.step()
        ring0.other_core()
        ring0.step((prep["ends"],))
        while ring0.left():
            ring0.other_core()
            ring0.step()
        ring0.other_core()
        weights0 = ring0.got, ring0.sib
    else:
        weights0 = gather_whole(piece0)
    own0, sib0 = weights0
    first_far = swap(after(first_rows, piece0), "tensor", 2)
    x = [[first_rows, first_sib, first_far, swap(first_far, "tensor", 1)]]
    far_in0 = far_swap(feedforward_in_weight[0], first_far, *sib0[:3])

    def ff_weights(far_in, far_out, *gate):
        return (
            feedforward_in_weight,
            feedforward_out_weight,
            in_sib,
            out_sib,
            far_in,
            [swap(after(v, *gate), "tensor", 1) for v in far_in],
            far_out,
            [swap(after(v, *gate), "tensor", 1) for v in far_out],
            x[0],
        )

    state0 = attention_forward(x[0], weights0, small[0])
    f1 = state0["f1"]
    piece1 = exchange_shards(1, True, (first_far, *sib0[:3]), own0[4:6])
    ring1 = RingGather(piece1) if pieces_fit else None
    if ring1:
        first = ring1.step((own0[-1],))
        ring1.other_core(f1)
        ring1.step((f1,))
    else:
        weights1, first = gather_whole(piece1), ()
    half = MODEL_WIDTH // 2
    far_in1 = [far_swap(feedforward_in_weight[1, :half], own0[-1])]
    ff_w = [ff_weights([far_in0], [], *first)]
    far_in1.append(far_swap(feedforward_in_weight[1, half:], far_in1[0]))
    ready = [far_in1[0], *(ring1.sib if ring1 else [])]
    state0.update(feedforward_forward(after(f1, *ready), weights0, ff_w[0], small[0], 0))
    z = state0["z"]
    x.append(gather_rows(z, far_in1[1]))
    if ring1:
        while ring1.left():
            ring1.step((z,))
        ring1.other_core(x[1][2])
        weights1 = ring1.got, ring1.sib
    ff_w.append(ff_weights(far_in1, [], x[1][2]))
    att_w = [weights0, weights1]
    saved = [state0, None]

    last = ENCODER_LAYERS - 1
    gs = [final_output_gradient]
    grads = [None] * ENCODER_LAYERS
    for l in reversed(range(ENCODER_LAYERS)):
        out = layer_backward(gs, x[l], att_w[l], ff_w[l], saved[l], small[l], l, l == last)
        if l == last:
            activations = out["z"]
        p3 = swap(out["p3"], "tensor", 1)
        p1 = swap(out["p1"], "tensor", 1)
        far = (out["p2"].astype(F32) + p3.astype(F32)).astype(BF16)
        p2 = swap(far, "tensor", 2)
        gs = [out["p0"], p1, p2]
        grads[l] = out["grads"]

    input_grad = sum(g.astype(F32) for g in gs).astype(BF16)
    both = jnp.stack(sum_all(after(grads[0], far), grads[1], p2))
    shape = (ENCODER_LAYERS, 2, ADAPTER_RANK, MODEL_WIDTH)
    grad_a = both[:, :16].reshape(shape).swapaxes(2, 3)
    grad_b = both[:, 16:].reshape(shape)
    return activations, input_grad, grad_a, grad_b


def solution(mesh):
    return jax.shard_map(
        body,
        mesh=mesh,
        in_specs=(
            P(("dp", "tensor"), None),
            P(("dp", "tensor"), None),
            P("dp", None),
            P(None, None, "dp", "tensor"),
            P(None, "dp", "tensor"),
            P(),
            P(),
            P(None, None, "tensor"),
            P(None, "tensor"),
            P(None, "tensor", None),
            P(),
            P(),
        ),
        out_specs=(P(("dp", "tensor"), None), P(("dp", "tensor"), None), P(), P()),
        check_vma=False,
    )
```
